32 devices in a mesh: nodes: 8 (over z, y), feat: 4 (over x, core).
Axes of the slice: x: 2, y: 2, z: 4, core: 2. Of those that a mesh axis runs over, the one named last changes fastest.
Arguments:
- features: bfloat16 [65536, 256], P('nodes', 'feat'), may hold values from -6 to 6
- degrees: int32 [65536], P('nodes'), may hold values from 1 to 16
- edge_weights: bfloat16 [2048, 128, 128], P('nodes'), may hold values from 0 to 0.099609375
- block_rows: int32 [2048], P('nodes'), may hold values from 0 to 63
- block_cols: int32 [2048], P('nodes'), may hold values from 0 to 111, as said below
- block_counts: int32 [8], P('nodes'), may hold values from 112 to 256, as said below
- send_lists: int32 [8, 3, 16], P('nodes'), may hold values from 0 to 63, as said below
- w_self: bfloat16 [256, 256], P(None, 'feat'), may hold values from -0.375 to 0.375
- w_neigh: bfloat16 [256, 256], P(None, 'feat'), may hold values from -0.375 to 0.375
- cotangent: bfloat16 [65536, 256], P('nodes', 'feat'), may hold values from -6 to 6
Outputs:
- mixed: bfloat16 [65536, 256], P('nodes', 'feat')
- grad_features: bfloat16 [65536, 256], P('nodes', 'feat')
- grad_self: float32 [256, 256], P(None, 'feat')
- grad_neigh: float32 [256, 256], P(None, 'feat')
The draws below stay inside these ranges and needn't reach their ends.
Inputs may be any that keep to these rules, and one draw needn't show every extreme that they name: `block_cols`: on each device, slots 0 to 111 name every extended block once; the other slots name any. A device uses its first block_counts slots. `send_lists`: the 16 entries of one device and level are distinct.
All inputs are finite; a program needn't handle non-finite values.
Results may differ from the reference program's by a relative error of at most 0.0065.
Values may be sent and summed in bfloat16 or wider, within the bound.
A program may use at most 192 MiB of HBM per device.

```python
import jax
import jax.numpy as jnp
from jax import lax

D = 256
BS = 128
RB = 64
SB = 16
LEVELS = 3
EXT = 112
NBLK = 256
NODES = 65536
BLOCKS = 2048
N_NODES = 8


def draw_block_cols(key, part):
    key = jax.random.fold_in(key, 5)
    device_keys = jax.random.split(key, N_NODES)

    def one_device(device_key):
        first_key, second_key = jax.random.split(device_key)
        covered = jax.random.permutation(first_key, EXT).astype(jnp.int32)
        extra_cols = jax.random.randint(second_key, (NBLK - EXT,), 0, EXT, dtype=jnp.int32)
        return jnp.concatenate([covered, extra_cols])
    return jax.vmap(one_device)(device_keys).reshape(BLOCKS).astype(jnp.int32)


def draw_block_counts(key, part):
    key = jax.random.fold_in(key, 7)
    count_key, pick_key = jax.random.split(key)
    counts = jax.random.randint(count_key, (N_NODES,), EXT, NBLK + 1, dtype=jnp.int32)
    lucky = jax.random.randint(pick_key, (), 0, N_NODES, dtype=jnp.int32)
    return jnp.where(jnp.arange(N_NODES, dtype=jnp.int32) == lucky, NBLK, counts).astype(jnp.int32)


def draw_send_lists(key, part):
    key = jax.random.fold_in(key, 9)
    device_keys = jax.random.split(key, N_NODES * LEVELS)

    def one_list(list_key):
        return jax.random.permutation(list_key, RB)[:SB].astype(jnp.int32)
    return jax.vmap(one_list)(device_keys).reshape(N_NODES, LEVELS, SB).astype(jnp.int32)


def plant(drawn, own_key, smallest, largest):
    shape = drawn.shape
    place = [jax.random.randint(jax.random.fold_in(own_key, axis), (), 0, shape[axis]) for axis in range(len(shape))]
    drawn = drawn.at[tuple(place)].set(smallest)
    longest = shape.index(max(shape))
    place[longest] = (place[longest] + 1) % shape[longest]
    return drawn.at[tuple(place)].set(largest)


def steps_of(rng, extent, shards, smallest, high):
    level = 1.0
    for position, shards_of in shards:
        steps = jax.random.uniform(jax.random.fold_in(jax.random.fold_in(rng, 6), position), (shards_of,), jnp.float32, smallest / len(shards), high / len(shards))
        level = level * jnp.repeat(jnp.exp(steps), extent[position] // shards_of).reshape((-1,) + (1,) * (len(extent) - 1 - position))
    return level


def gaussian(key, shape, width, limit, cuts=(), kind=jnp.bfloat16):
    entries = width * jax.random.normal(key, shape, jnp.float32)
    if cuts:
        entries = entries * steps_of(key, shape, cuts, -0.22, 0.18)
    return jnp.clip(entries, -limit, limit).astype(kind)


def setup_inputs(seed: int = 0) -> dict:
    splits = jax.random.split(jax.random.key(seed), 11)
    features = gaussian(splits[0], (NODES, D), 1.0, 6.0, ((0, 8), (1, 4)))
    degrees = plant(jax.random.randint(splits[1], (NODES,), 1, 17), jax.random.fold_in(splits[1], 1), 1, 16).astype(jnp.int32)
    edge_weights = jnp.clip(0.099609375 * jax.random.uniform(splits[2], (BLOCKS, BS, BS), jnp.float32) ** steps_of(splits[2], (BLOCKS, BS, BS), ((0, 8),), -0.2, 0.2), 0.0, 0.099609375).astype(jnp.bfloat16)
    block_rows = plant(jax.random.randint(splits[3], (BLOCKS,), 0, RB), jax.random.fold_in(splits[3], 1), 0, RB - 1).astype(jnp.int32)
    block_cols = draw_block_cols(jax.random.fold_in(splits[10], 71), 0)
    block_counts = draw_block_counts(jax.random.fold_in(splits[10], 71), 0)
    send_lists = draw_send_lists(jax.random.fold_in(splits[10], 71), 0)
    w_self = gaussian(splits[7], (D, D), D ** -0.5, 0.375, ((1, 4),))
    w_neigh = gaussian(splits[8], (D, D), D ** -0.5, 0.375, ((1, 4),))
    cotangent = gaussian(splits[9], (NODES, D), 1.0, 6.0, ((0, 8), (1, 4)))
    return dict(features=features, degrees=degrees, edge_weights=edge_weights, block_rows=block_rows, block_cols=block_cols, block_counts=block_counts, send_lists=send_lists, w_self=w_self, w_neigh=w_neigh, cotangent=cotangent)


gelu_scale = 0.7978845608028654
gelu_cubic = 0.044715


def gelu_value(values):
    inner = gelu_scale * (values + gelu_cubic * values * values * values)
    return 0.5 * values * (1.0 + jnp.tanh(inner))


def gelu_slope(values):
    inner = gelu_scale * (values + gelu_cubic * values * values * values)
    tanh_inner = jnp.tanh(inner)
    return 0.5 * (1.0 + tanh_inner) + 0.5 * values * (1.0 - tanh_inner * tanh_inner) * gelu_scale * (1.0 + 3.0 * gelu_cubic * values * values)


def reference(features, degrees, edge_weights, block_rows, block_cols, block_counts, send_lists, w_self, w_neigh, cotangent):
    feature_blocks = features.reshape(N_NODES, RB, BS, D)
    weight_blocks = edge_weights.reshape(N_NODES, NBLK, BS, BS)
    row_table = block_rows.reshape(N_NODES, NBLK)
    col_table = block_cols.reshape(N_NODES, NBLK)
    inverse = (1.0 / degrees.astype(jnp.float32)).reshape(N_NODES, RB, BS, 1)
    slot_index = jnp.arange(NBLK, dtype=jnp.int32)
    devices = jnp.arange(N_NODES, dtype=jnp.int32)

    def selector(targets, device, total):
        active = slot_index < block_counts[device]
        match = targets[None, :] == jnp.arange(total, dtype=jnp.int32)[:, None]
        return (match & active[None, :]).astype(jnp.float32)

    def forward_one(device):
        parts = [feature_blocks[device]]
        for level in range(LEVELS):
            partner = jnp.bitwise_xor(device, 1 << level)
            parts.append(jnp.take(feature_blocks[partner], send_lists[partner, level], axis=0))
        table = jnp.concatenate(parts, axis=0)
        picked = jnp.take(table, col_table[device], axis=0).astype(jnp.float32)
        product = jnp.einsum("sij,sjf->sif", weight_blocks[device].astype(jnp.float32), picked)
        onehot = selector(row_table[device], device, RB)
        summed = jnp.dot(onehot, product.reshape(NBLK, BS * D), precision=lax.Precision.HIGHEST).reshape(RB, BS, D)
        return (summed * inverse[device]).astype(jnp.bfloat16)

    aggregated = lax.map(forward_one, devices).reshape(N_NODES * RB * BS, D)
    preact = jnp.dot(features, w_self, preferred_element_type=jnp.float32) + jnp.dot(aggregated, w_neigh, preferred_element_type=jnp.float32)
    mixed = gelu_value(preact).astype(jnp.bfloat16)
    pre_grad = (cotangent.astype(jnp.float32) * gelu_slope(preact)).astype(jnp.bfloat16)
    grad_self = jnp.dot(features.T, pre_grad, preferred_element_type=jnp.float32)
    grad_neigh = jnp.dot(aggregated.T, pre_grad, preferred_element_type=jnp.float32)
    direct_blocks = jnp.dot(pre_grad, w_self.T, preferred_element_type=jnp.float32).reshape(N_NODES, RB, BS, D)
    scaled = (jnp.dot(pre_grad, w_neigh.T, preferred_element_type=jnp.float32).reshape(N_NODES, RB, BS, D) * inverse).astype(jnp.bfloat16)

    def backward_one(device):
        picked = jnp.take(scaled[device], row_table[device], axis=0).astype(jnp.float32)
        product = jnp.einsum("sji,sjf->sif", weight_blocks[device].astype(jnp.float32), picked)
        onehot = selector(col_table[device], device, EXT)
        spread = jnp.dot(onehot, product.reshape(NBLK, BS * D), precision=lax.Precision.HIGHEST).reshape(EXT, BS, D)
        return spread[:RB] + direct_blocks[device], spread[RB:]

    own_part, border_part = lax.map(backward_one, devices)

    def collect_one(device):
        total = own_part[device]
        for level in range(LEVELS):
            partner = jnp.bitwise_xor(device, 1 << level)
            piece = lax.dynamic_slice_in_dim(border_part[partner], level * SB, SB, 0)
            total = total.at[send_lists[device, level]].add(piece)
        return total.astype(jnp.bfloat16)

    grad_features = lax.map(collect_one, devices).reshape(N_NODES * RB * BS, D)
    return (mixed, grad_features, grad_self, grad_neigh)
```

```python
import functools

import jax
import jax.numpy as jnp
from jax import lax
from jax.experimental import pallas as pl
from jax.experimental.pallas import tpu as pltpu
from jax.sharding import PartitionSpec as P

gelu_scale = 0.7978845608028654
gelu_cubic = 0.044715
GROUP = 4
SMEM = pl.BlockSpec(memory_space=pltpu.SMEM)
VMEM = pl.BlockSpec(memory_space=pltpu.VMEM)
PARAMS = pltpu.CompilerParams(vmem_limit_bytes=56 * 1024 * 1024)
NT = (((1,), (1,)), ((), ()))


def partner(value, axis, apart):
    return lax.ppermute(value, axis, [(i, i ^ 1 << apart) for i in range(lax.axis_size(axis))])


def lanes(index, size):
    return pl.ds(pl.multiple_of(index * size, size), size)


def for_slots(first, last, order_ref, product, store):
    groups = (last - first) // GROUP

    def several(step, carry):
        slots = [order_ref[first + step * GROUP + k] for k in range(GROUP)]
        values = [product(slot) for slot in slots]
        for slot, value in zip(slots, values):
            store(slot, value)
        return carry

    def single(step, carry):
        slot = order_ref[step]
        store(slot, product(slot))
        return carry

    lax.fori_loop(0, groups, several, 0)
    lax.fori_loop(first + groups * GROUP, last, single, 0)


def pack_kernel(own_blocks, cols_ref, count_ref, sends_ref, table_ref, order_ref, split_ref, *piece_refs):
    size = piece_refs[0].shape[2]
    for level, piece_ref in enumerate(piece_refs):
        for j in range(piece_ref.shape[0]):
            piece_ref[j] = table_ref[:, lanes(sends_ref[level, j], size)]
    count = count_ref[0]

    def place(slot, state):
        low, high = state
        own = cols_ref[slot] < own_blocks
        order_ref[jnp.where(own, low, high)] = slot
        return jnp.where(own, low + 1, low), jnp.where(own, high, high - 1)

    low, _ = lax.fori_loop(0, count, place, (jnp.int32(0), count - 1))
    split_ref[0] = low
    split_ref[1] = count


def gather_own_kernel(rows_ref, cols_ref, order_ref, split_ref, weight_ref, table_ref, total_ref):
    size = weight_ref.shape[1]
    total_ref[...] = jnp.zeros_like(total_ref)

    def product(slot):
        block = table_ref[:, lanes(cols_ref[slot], size)]
        return lax.dot_general(block, weight_ref[slot], NT, preferred_element_type=jnp.float32)

    def store(slot, value):
        total_ref[:, lanes(rows_ref[slot], size)] += value

    for_slots(0, split_ref[0], order_ref, product, store)


def gather_border_kernel(
    own_blocks, rows_ref, cols_ref, order_ref, split_ref, weight_ref, total_ref, inverse_ref, *rest
):
    piece_refs, out_ref, border_ref, sum_ref = rest[:-3], rest[-3], rest[-2], rest[-1]
    size = weight_ref.shape[1]
    border_size = piece_refs[0].shape[0]
    for level, piece_ref in enumerate(piece_refs):
        border_ref[level * border_size : (level + 1) * border_size] = piece_ref[...]
    sum_ref[...] = total_ref[...]

    def product(slot):
        block = border_ref[cols_ref[slot] - own_blocks]
        return lax.dot_general(block, weight_ref[slot], NT, preferred_element_type=jnp.float32)

    def store(slot, value):
        sum_ref[:, lanes(rows_ref[slot], size)] += value

    for_slots(split_ref[0], split_ref[1], order_ref, product, store)
    out_ref[...] = (sum_ref[...] * inverse_ref[...]).astype(jnp.bfloat16)


def dense_kernel(
    own_ref, agg_ref, self_ref, neigh_ref, cot_ref, mixed_ref, grad_ref, grad_self_ref, grad_neigh_ref
):
    @pl.when(pl.program_id(0) == 0)
    def _():
        grad_self_ref[...] = jnp.zeros_like(grad_self_ref)
        grad_neigh_ref[...] = jnp.zeros_like(grad_neigh_ref)

    rows, agg = own_ref[...], agg_ref[...]
    values = jnp.dot(self_ref[...], rows, preferred_element_type=jnp.float32) + jnp.dot(
        neigh_ref[...], agg, preferred_element_type=jnp.float32
    )
    square = values * values
    tanh_inner = jnp.tanh(gelu_scale * (values + gelu_cubic * square * values))
    half = 0.5 * (1.0 + tanh_inner)
    mixed_ref[...] = (values * half).astype(jnp.bfloat16)
    slope = half + 0.5 * values * (1.0 - tanh_inner * tanh_inner) * gelu_scale * (
        1.0 + 3.0 * gelu_cubic * square
    )
    grad = (cot_ref[...].astype(jnp.float32) * slope).astype(jnp.bfloat16)
    grad_ref[...] = grad
    grad_self_ref[...] += lax.dot_general(grad, rows, NT, preferred_element_type=jnp.float32)
    grad_neigh_ref[...] += lax.dot_general(grad, agg, NT, preferred_element_type=jnp.float32)


def spread_border_kernel(
    own_blocks, rows_ref, cols_ref, order_ref, split_ref, weight_ref, whole_ref, self_ref, neigh_ref,
    inverse_ref, direct_ref, scaled_ref, *rest
):
    piece_refs, border_ref = rest[:-1], rest[-1]
    size = weight_ref.shape[1]
    chunk = 8 * size

    def dense(step, carry):
        part = lanes(step, chunk)
        grad = whole_ref[:, part]
        direct_ref[:, part] = jnp.dot(self_ref[...], grad, preferred_element_type=jnp.float32)
        scaled = jnp.dot(neigh_ref[...], grad, preferred_element_type=jnp.float32)
        scaled_ref[:, part] = (scaled * inverse_ref[:, part]).astype(jnp.bfloat16)
        return carry

    lax.fori_loop(0, whole_ref.shape[1] // chunk, dense, 0)
    border_ref[...] = jnp.zeros_like(border_ref)

    def product(slot):
        block = scaled_ref[:, lanes(rows_ref[slot], size)]
        return jnp.dot(block, weight_ref[slot], preferred_element_type=jnp.float32)

    def store(slot, value):
        border_ref[cols_ref[slot] - own_blocks] += value

    for_slots(split_ref[0], split_ref[1], order_ref, product, store)
    border_size = piece_refs[0].shape[0]
    for level, piece_ref in enumerate(piece_refs):
        piece_ref[...] = border_ref[level * border_size : (level + 1) * border_size].astype(jnp.bfloat16)


def spread_own_kernel(
    rows_ref, cols_ref, order_ref, split_ref, weight_ref, scaled_ref, direct_ref, total_ref
):
    size = weight_ref.shape[1]
    total_ref[...] = direct_ref[...]

    def product(slot):
        block = scaled_ref[:, lanes(rows_ref[slot], size)]
        return jnp.dot(block, weight_ref[slot], preferred_element_type=jnp.float32)

    def store(slot, value):
        total_ref[:, lanes(cols_ref[slot], size)] += value

    for_slots(0, split_ref[0], order_ref, product, store)


def collect_kernel(sends_ref, total_ref, *rest):
    piece_refs, out_ref, sum_ref = rest[:-2], rest[-2], rest[-1]
    size = piece_refs[0].shape[2]
    sum_ref[...] = total_ref[...]
    for level, piece_ref in enumerate(piece_refs):
        for j in range(piece_ref.shape[0]):
            sum_ref[:, lanes(sends_ref[level, j], size)] += piece_ref[j].astype(jnp.float32)
    out_ref[...] = sum_ref[...].astype(jnp.bfloat16)


def local(
    features,
    degrees,
    edge_weights,
    block_rows,
    block_cols,
    block_counts,
    send_lists,
    w_self,
    w_neigh,
    cotangent,
):
    row_count, width = features.shape
    slot_count, size, _ = edge_weights.shape
    own_blocks = row_count // size
    border_size = send_lists.shape[2]
    levels = send_lists.shape[1]
    hidden = w_self.shape[0]
    shape = jax.ShapeDtypeStruct
    bf16, f32, i32 = jnp.bfloat16, jnp.float32, jnp.int32
    piece = shape((border_size, width, size), bf16)
    inverse = (1.0 / degrees.astype(f32))[None, :]
    own = features.T
    whole_rows = lax.all_gather(own, "feat", axis=0, tiled=True)
    both = jnp.concatenate([w_self.T, w_neigh.T], axis=1)
    whole_both = lax.all_gather(both, "feat", axis=0, tiled=True)
    start_row = lax.axis_index("feat") * width
    rows_self = lax.dynamic_slice_in_dim(whole_both, start_row, width, 1).T
    rows_neigh = lax.dynamic_slice_in_dim(whole_both, hidden + start_row, width, 1).T
    sends = send_lists[0]

    order, split, *pieces = pl.pallas_call(
        functools.partial(pack_kernel, own_blocks),
        out_shape=[shape((slot_count,), i32), shape((2,), i32)] + [piece] * levels,
        in_specs=[SMEM, SMEM, SMEM, VMEM],
        out_specs=[SMEM, SMEM] + [VMEM] * levels,
        compiler_params=PARAMS,
        name="pack",
    )(block_cols, block_counts, sends, own)
    tables = (block_rows, block_cols, order, split)
    arrived = [partner(value, "nodes", level) for level, value in enumerate(pieces)]
    total = pl.pallas_call(
        gather_own_kernel,
        out_shape=shape((width, row_count), f32),
        in_specs=[SMEM] * 4 + [VMEM] * 2,
        out_specs=VMEM,
        compiler_params=PARAMS,
        cost_estimate=pl.CostEstimate(flops=4 * 10**9, bytes_accessed=12 * 10**6, transcendentals=0),
        name="gather_own",
    )(*tables, edge_weights, own)
    aggregated = pl.pallas_call(
        functools.partial(gather_border_kernel, own_blocks),
        out_shape=shape((width, row_count), bf16),
        in_specs=[SMEM] * 4 + [VMEM] * (3 + levels),
        out_specs=VMEM,
        scratch_shapes=[
            pltpu.VMEM((levels * border_size, width, size), bf16),
            pltpu.VMEM((width, row_count), f32),
        ],
        compiler_params=PARAMS,
        name="gather_border",
    )(*tables, edge_weights, total, inverse, *arrived)
    whole_agg = lax.all_gather(aggregated, "feat", axis=0, tiled=True)

    chunk = 8 * size
    steps = row_count // chunk
    column = pl.BlockSpec((width, chunk), lambda i: (0, i))
    tall = pl.BlockSpec((hidden, chunk), lambda i: (0, i))
    fixed = pl.BlockSpec((width, hidden), lambda i: (0, 0))
    mixed, pre_grad, grad_self, grad_neigh = pl.pallas_call(
        dense_kernel,
        grid=(steps,),
        out_shape=[shape((width, row_count), bf16)] * 2 + [shape((width, hidden), f32)] * 2,
        in_specs=[tall, tall, fixed, fixed, column],
        out_specs=[column, column, fixed, fixed],
        compiler_params=PARAMS,
        name="dense",
    )(whole_rows, whole_agg, w_self.T, w_neigh.T, cotangent.T)
    whole_grad = lax.all_gather(pre_grad, "feat", axis=0, tiled=True)
    grad_self, grad_neigh = lax.psum((grad_self, grad_neigh), "nodes")

    direct, scaled, *pieces = pl.pallas_call(
        functools.partial(spread_border_kernel, own_blocks),
        out_shape=[shape((width, row_count), f32), shape((width, row_count), bf16)] + [piece] * levels,
        in_specs=[SMEM] * 4 + [VMEM] * 5,
        out_specs=[VMEM] * (2 + levels),
        scratch_shapes=[pltpu.VMEM((levels * border_size, width, size), f32)],
        compiler_params=PARAMS,
        name="spread_border",
    )(*tables, edge_weights, whole_grad, rows_self, rows_neigh, inverse)
    returned = [partner(value, "nodes", level) for level, value in enumerate(pieces)]
    total = pl.pallas_call(
        spread_own_kernel,
        out_shape=shape((width, row_count), f32),
        in_specs=[SMEM] * 4 + [VMEM] * 3,
        out_specs=VMEM,
        compiler_params=PARAMS,
        cost_estimate=pl.CostEstimate(flops=4 * 10**9, bytes_accessed=12 * 10**6, transcendentals=0),
        name="spread_own",
    )(*tables, edge_weights, scaled, direct)
    grad_features = pl.pallas_call(
        collect_kernel,
        out_shape=shape((width, row_count), bf16),
        in_specs=[SMEM] + [VMEM] * (1 + levels),
        out_specs=VMEM,
        scratch_shapes=[pltpu.VMEM((width, row_count), f32)],
        compiler_params=PARAMS,
        name="collect",
    )(sends, total, *returned)
    return (mixed.T, grad_features.T, grad_self.T, grad_neigh.T)


def solution(mesh):
    in_specs = (
        P("nodes", "feat"),
        P("nodes"),
        P("nodes", None, None),
        P("nodes"),
        P("nodes"),
        P("nodes"),
        P("nodes", None, None),
        P(None, "feat"),
        P(None, "feat"),
        P("nodes", "feat"),
    )
    out_specs = (P("nodes", "feat"), P("nodes", "feat"), P(None, "feat"), P(None, "feat"))
    return jax.shard_map(local, mesh=mesh, in_specs=in_specs, out_specs=out_specs, check_vma=False)
```

```python
import functools

import jax
import jax.numpy as jnp
from jax import lax
from jax.experimental import pallas as pl
from jax.experimental.pallas import tpu as pltpu
from jax.sharding import PartitionSpec as P

gelu_scale = 0.7978845608028654
gelu_cubic = 0.044715
GROUP = 8
SMEM = pl.BlockSpec(memory_space=pltpu.SMEM)
VMEM = pl.BlockSpec(memory_space=pltpu.VMEM)
PARAMS = pltpu.CompilerParams(vmem_limit_bytes=56 * 1024 * 1024)
NT = (((1,), (1,)), ((), ()))


def partner(value, axis, apart):
    return lax.ppermute(value, axis, [(i, i ^ 1 << apart) for i in range(lax.axis_size(axis))])


def lanes(index, size):
    return pl.ds(pl.multiple_of(index * size, size), size)


def for_slots(first, last, order_ref, product, store):
    groups = (last - first) // GROUP

    def several(step, carry):
        slots = [order_ref[first + step * GROUP + k] for k in range(GROUP)]
        values = [product(slot) for slot in slots]
        for slot, value in zip(slots, values):
            store(slot, value)
        return carry

    def single(step, carry):
        slot = order_ref[step]
        store(slot, product(slot))
        return carry

    lax.fori_loop(0, groups, several, 0)
    lax.fori_loop(first + groups * GROUP, last, single, 0)


def pack_kernel(own_blocks, cols_ref, count_ref, sends_ref, table_ref, order_ref, split_ref, *piece_refs):
    size = piece_refs[0].shape[2]
    for level, piece_ref in enumerate(piece_refs):
        for j in range(piece_ref.shape[0]):
            piece_ref[j] = table_ref[:, lanes(sends_ref[level, j], size)]
    count = count_ref[0]

    def place(slot, state):
        low, high = state
        own = cols_ref[slot] < own_blocks
        order_ref[jnp.where(own, low, high)] = slot
        return jnp.where(own, low + 1, low), jnp.where(own, high, high - 1)

    low, _ = lax.fori_loop(0, count, place, (jnp.int32(0), count - 1))
    split_ref[0] = low
    split_ref[1] = count


def gather_own_kernel(rows_ref, cols_ref, order_ref, split_ref, weight_ref, table_ref, total_ref):
    size = weight_ref.shape[1]
    total_ref[...] = jnp.zeros_like(total_ref)

    def product(slot):
        block = table_ref[:, lanes(cols_ref[slot], size)]
        return lax.dot_general(block, weight_ref[slot], NT, preferred_element_type=jnp.float32)

    def store(slot, value):
        total_ref[:, lanes(rows_ref[slot], size)] += value

    for_slots(0, split_ref[0], order_ref, product, store)


def gather_border_kernel(
    own_blocks, rows_ref, cols_ref, order_ref, split_ref, weight_ref, total_ref, inverse_ref, *rest
):
    piece_refs, out_ref, border_ref, sum_ref = rest[:-3], rest[-3], rest[-2], rest[-1]
    size = weight_ref.shape[1]
    border_size = piece_refs[0].shape[0]
    for level, piece_ref in enumerate(piece_refs):
        border_ref[level * border_size : (level + 1) * border_size] = piece_ref[...]
    sum_ref[...] = total_ref[...]

    def product(slot):
        block = border_ref[cols_ref[slot] - own_blocks]
        return lax.dot_general(block, weight_ref[slot], NT, preferred_element_type=jnp.float32)

    def store(slot, value):
        sum_ref[:, lanes(rows_ref[slot], size)] += value

    for_slots(split_ref[0], split_ref[1], order_ref, product, store)
    out_ref[...] = (sum_ref[...] * inverse_ref[...]).astype(jnp.bfloat16)


def middle_kernel(
    levels, chunk, whole_ref, agg_ref, self_ref, neigh_ref, slab_ref, cot_ref, inverse_ref,
    mixed_ref, direct_ref, scaled_ref, sums_ref,
    all_agg, all_grad, slabs, back_ref, partial_ref, arrived_ref,
    gather_send, gather_recv, slab_send, slab_recv, sum_send, sum_recv,
):
    width, nodes = agg_ref.shape
    steps = nodes // chunk
    me, node = lax.axis_index("feat"), lax.axis_index("nodes")
    near = me + 1 - 2 * (me % 2)
    cross = (me + 2) % 4
    far = 3 - me
    mates = [node + (1 << level) * (1 - 2 * ((node // (1 << level)) % 2)) for level in range(levels)]

    def rows(owner):
        return pl.ds(pl.multiple_of(owner * width, width), width)

    def moved(table, phase, kind, owner, step, target):
        view = table.at[rows(owner), lanes(step, chunk)]
        return pltpu.make_async_remote_copy(
            src_ref=view,
            dst_ref=view,
            send_sem=gather_send.at[phase, kind, step],
            recv_sem=gather_recv.at[phase, kind, step],
            device_id={"feat": target},
            device_id_type=pl.DeviceIdType.MESH,
        )

    def slab(kind, target):
        return pltpu.make_async_remote_copy(
            src_ref=slab_ref.at[target],
            dst_ref=slabs.at[me],
            send_sem=slab_send.at[kind],
            recv_sem=slab_recv.at[kind],
            device_id={"feat": target},
            device_id_type=pl.DeviceIdType.MESH,
        )

    def summed(level):
        return pltpu.make_async_remote_copy(
            src_ref=partial_ref.at[level],
            dst_ref=arrived_ref.at[level],
            send_sem=sum_send.at[level],
            recv_sem=sum_recv.at[level],
            device_id={"nodes": mates[level]},
            device_id_type=pl.DeviceIdType.MESH,
        )

    def share(table, phase, step):
        moved(table, phase, 0, me, step, cross).start()
        moved(table, phase, 1, me, step, near).start()

    def forward(table, phase, step):
        moved(table, phase, 0, cross, step, cross).wait_recv()
        moved(table, phase, 2, cross, step, near).start()

    def complete(table, phase, step):
        moved(table, phase, 1, near, step, near).wait_recv()
        moved(table, phase, 2, far, step, near).wait_recv()

    barrier = pltpu.get_barrier_semaphore()
    for target in (near, cross, far):
        pl.semaphore_signal(
            barrier, inc=1, device_id={"feat": target}, device_id_type=pl.DeviceIdType.MESH
        )
    for mate in mates:
        pl.semaphore_signal(
            barrier, inc=1, device_id={"nodes": mate}, device_id_type=pl.DeviceIdType.MESH
        )
    all_agg[rows(me), :] = agg_ref[...]
    slabs[me] = slab_ref[me]
    partial_ref[0] = jnp.zeros(partial_ref.shape[1:], jnp.float32)
    pl.semaphore_wait(barrier, 3 + levels)

    def share_agg(step, carry):
        share(all_agg, 0, step)
        return carry

    lax.fori_loop(0, steps, share_agg, 0)
    for kind, target in enumerate((near, cross, far)):
        slab(kind, target).start()

    def dense(step):
        complete(all_agg, 0, step)
        part = lanes(step, chunk)
        whole, agg = whole_ref[:, part], all_agg[:, part]
        values = jnp.dot(self_ref[...], whole, preferred_element_type=jnp.float32) + jnp.dot(
            neigh_ref[...], agg, preferred_element_type=jnp.float32
        )
        square = values * values
        tanh_inner = jnp.tanh(gelu_scale * (values + gelu_cubic * square * values))
        half = 0.5 * (1.0 + tanh_inner)
        mixed_ref[:, part] = (values * half).astype(jnp.bfloat16)
        slope = half + 0.5 * values * (1.0 - tanh_inner * tanh_inner) * gelu_scale * (
            1.0 + 3.0 * gelu_cubic * square
        )
        grad = (cot_ref[:, part].astype(jnp.float32) * slope).astype(jnp.bfloat16)
        all_grad[rows(me), part] = grad
        share(all_grad, 1, step)
        partial_ref[0, 0] += lax.dot_general(grad, whole, NT, preferred_element_type=jnp.float32)
        partial_ref[0, 1] += lax.dot_general(grad, agg, NT, preferred_element_type=jnp.float32)

    def dense_step(step, carry):
        forward(all_agg, 0, step + 1)
        dense(step)
        return carry

    forward(all_agg, 0, 0)
    lax.fori_loop(0, steps - 1, dense_step, 0)
    dense(steps - 1)

    for kind, target in enumerate((near, cross, far)):
        slab(kind, target).wait_recv()
    back_ref[...] = slabs[...].reshape(back_ref.shape[1], back_ref.shape[0]).T

    def project(step):
        complete(all_grad, 1, step)
        part = lanes(step, chunk)
        both = jnp.dot(back_ref[...], all_grad[:, part], preferred_element_type=jnp.float32)
        direct_ref[:, part] = both[:width]
        scaled_ref[:, part] = (both[width:] * inverse_ref[:, part]).astype(jnp.bfloat16)

    def project_step(step, carry):
        forward(all_grad, 1, step + 1)
        project(step)
        return carry

    forward(all_grad, 1, 0)
    for level in range(levels):
        summed(level).start()
        lax.fori_loop(
            level * (steps - 1) // levels, (level + 1) * (steps - 1) // levels, project_step, 0
        )
        summed(level).wait_recv()
        partial_ref[level + 1] = partial_ref[level] + arrived_ref[level]
    sums_ref[...] = partial_ref[levels]
    project(steps - 1)

    def finish(step, carry):
        for phase, table in enumerate((all_agg, all_grad)):
            moved(table, phase, 0, me, step, cross).wait_send()
            moved(table, phase, 1, me, step, near).wait_send()
            moved(table, phase, 2, cross, step, near).wait_send()
        return carry

    lax.fori_loop(0, steps, finish, 0)
    for kind, target in enumerate((near, cross, far)):
        slab(kind, target).wait_send()
    for level in range(levels):
        summed(level).wait_send()


def spread_border_kernel(
    own_blocks, rows_ref, cols_ref, order_ref, split_ref, weight_ref, scaled_ref, *rest
):
    piece_refs, border_ref = rest[:-1], rest[-1]
    size = weight_ref.shape[1]
    border_ref[...] = jnp.zeros_like(border_ref)

    def product(slot):
        block = scaled_ref[:, lanes(rows_ref[slot], size)]
        return jnp.dot(block, weight_ref[slot], preferred_element_type=jnp.float32)

    def store(slot, value):
        border_ref[cols_ref[slot] - own_blocks] += value

    for_slots(split_ref[0], split_ref[1], order_ref, product, store)
    border_size = piece_refs[0].shape[0]
    for level, piece_ref in enumerate(piece_refs):
        piece_ref[...] = border_ref[level * border_size : (level + 1) * border_size].astype(jnp.bfloat16)


def spread_own_kernel(
    rows_ref, cols_ref, order_ref, split_ref, weight_ref, scaled_ref, direct_ref, total_ref
):
    size = weight_ref.shape[1]
    total_ref[...] = direct_ref[...]

    def product(slot):
        block = scaled_ref[:, lanes(rows_ref[slot], size)]
        return jnp.dot(block, weight_ref[slot], preferred_element_type=jnp.float32)

    def store(slot, value):
        total_ref[:, lanes(cols_ref[slot], size)] += value

    for_slots(0, split_ref[0], order_ref, product, store)


def collect_kernel(sends_ref, total_ref, *rest):
    piece_refs, out_ref, sum_ref = rest[:-2], rest[-2], rest[-1]
    size = piece_refs[0].shape[2]
    sum_ref[...] = total_ref[...]
    for level, piece_ref in enumerate(piece_refs):
        for j in range(piece_ref.shape[0]):
            sum_ref[:, lanes(sends_ref[level, j], size)] += piece_ref[j].astype(jnp.float32)
    out_ref[...] = sum_ref[...].astype(jnp.bfloat16)


def local(
    features,
    degrees,
    edge_weights,
    block_rows,
    block_cols,
    block_counts,
    send_lists,
    w_self,
    w_neigh,
    cotangent,
):
    row_count, width = features.shape
    slot_count, size, _ = edge_weights.shape
    own_blocks = row_count // size
    border_size = send_lists.shape[2]
    levels = send_lists.shape[1]
    hidden = w_self.shape[0]
    shape = jax.ShapeDtypeStruct
    bf16, f32, i32 = jnp.bfloat16, jnp.float32, jnp.int32
    piece = shape((border_size, width, size), bf16)
    inverse = (1.0 / degrees.astype(f32))[None, :]
    own = features.T
    whole_rows = lax.all_gather(own, "feat", axis=0, tiled=True)
    groups = hidden // width
    slab = jnp.concatenate(
        [w.T.reshape(width, groups, width).transpose(1, 0, 2) for w in (w_self, w_neigh)], axis=2
    )
    sends = send_lists[0]

    order, split, *pieces = pl.pallas_call(
        functools.partial(pack_kernel, own_blocks),
        out_shape=[shape((slot_count,), i32), shape((2,), i32)] + [piece] * levels,
        in_specs=[SMEM, SMEM, SMEM, VMEM],
        out_specs=[SMEM, SMEM] + [VMEM] * levels,
        compiler_params=PARAMS,
        name="pack",
    )(block_cols, block_counts, sends, own)
    tables = (block_rows, block_cols, order, split)
    arrived = [partner(value, "nodes", level) for level, value in enumerate(pieces)]
    total = pl.pallas_call(
        gather_own_kernel,
        out_shape=shape((width, row_count), f32),
        in_specs=[SMEM] * 4 + [VMEM] * 2,
        out_specs=VMEM,
        compiler_params=PARAMS,
        cost_estimate=pl.CostEstimate(flops=4 * 10**9, bytes_accessed=12 * 10**6, transcendentals=0),
        name="gather_own",
    )(*tables, edge_weights, own)
    aggregated = pl.pallas_call(
        functools.partial(gather_border_kernel, own_blocks),
        out_shape=shape((width, row_count), bf16),
        in_specs=[SMEM] * 4 + [VMEM] * (3 + levels),
        out_specs=VMEM,
        scratch_shapes=[
            pltpu.VMEM((levels * border_size, width, size), bf16),
            pltpu.VMEM((width, row_count), f32),
        ],
        compiler_params=PARAMS,
        name="gather_border",
    )(*tables, edge_weights, total, inverse, *arrived)

    chunk = 8 * size
    steps = row_count // chunk
    dma = pltpu.SemaphoreType.DMA
    mixed, direct, scaled, sums = pl.pallas_call(
        functools.partial(middle_kernel, levels, chunk),
        out_shape=[
            shape((width, row_count), bf16),
            shape((width, row_count), f32),
            shape((width, row_count), bf16),
            shape((2, width, hidden), f32),
        ],
        in_specs=[VMEM] * 7,
        out_specs=[VMEM] * 4,
        scratch_shapes=[
            pltpu.VMEM((hidden, row_count), bf16),
            pltpu.VMEM((hidden, row_count), bf16),
            pltpu.VMEM((groups, width, 2 * width), bf16),
            pltpu.VMEM((2 * width, hidden), bf16),
            pltpu.VMEM((levels + 1, 2, width, hidden), f32),
            pltpu.VMEM((levels, 2, width, hidden), f32),
            dma((2, 3, steps)),
            dma((2, 3, steps)),
            dma((3,)),
            dma((3,)),
            dma((levels,)),
            dma((levels,)),
        ],
        compiler_params=pltpu.CompilerParams(
            vmem_limit_bytes=56 * 1024 * 1024, collective_id=0, has_side_effects=True
        ),
        name="middle",
    )(whole_rows, aggregated, w_self.T, w_neigh.T, slab, cotangent.T, inverse)
    grad_self, grad_neigh = sums[0], sums[1]

    pieces = pl.pallas_call(
        functools.partial(spread_border_kernel, own_blocks),
        out_shape=[piece] * levels,
        in_specs=[SMEM] * 4 + [VMEM] * 2,
        out_specs=[VMEM] * levels,
        scratch_shapes=[pltpu.VMEM((levels * border_size, width, size), f32)],
        compiler_params=PARAMS,
        name="spread_border",
    )(*tables, edge_weights, scaled)
    returned = [partner(value, "nodes", level) for level, value in enumerate(pieces)]
    total = pl.pallas_call(
        spread_own_kernel,
        out_shape=shape((width, row_count), f32),
        in_specs=[SMEM] * 4 + [VMEM] * 3,
        out_specs=VMEM,
        compiler_params=PARAMS,
        cost_estimate=pl.CostEstimate(flops=4 * 10**9, bytes_accessed=12 * 10**6, transcendentals=0),
        name="spread_own",
    )(*tables, edge_weights, scaled, direct)
    grad_features = pl.pallas_call(
        collect_kernel,
        out_shape=shape((width, row_count), bf16),
        in_specs=[SMEM] + [VMEM] * (1 + levels),
        out_specs=VMEM,
        scratch_shapes=[pltpu.VMEM((width, row_count), f32)],
        compiler_params=PARAMS,
        name="collect",
    )(sends, total, *returned)
    return (mixed.T, grad_features.T, grad_self.T, grad_neigh.T)


def solution(mesh):
    in_specs = (
        P("nodes", "feat"),
        P("nodes"),
        P("nodes", None, None),
        P("nodes"),
        P("nodes"),
        P("nodes"),
        P("nodes", None, None),
        P(None, "feat"),
        P(None, "feat"),
        P("nodes", "feat"),
    )
    out_specs = (P("nodes", "feat"), P("nodes", "feat"), P(None, "feat"), P(None, "feat"))
    return jax.shard_map(local, mesh=mesh, in_specs=in_specs, out_specs=out_specs, check_vma=False)
```

```python
import functools

import jax
import jax.numpy as jnp
from jax import lax
from jax.experimental import pallas as pl
from jax.experimental.pallas import tpu as pltpu
from jax.sharding import PartitionSpec as P

gelu_scale = 0.7978845608028654
gelu_cubic = 0.044715
GROUP = 16
TAIL = 4
PARTS = 4
SMEM = pl.BlockSpec(memory_space=pltpu.SMEM)
VMEM = pl.BlockSpec(memory_space=pltpu.VMEM)
ANY = pl.BlockSpec(memory_space=pl.ANY)
PARAMS = pltpu.CompilerParams(vmem_limit_bytes=56 * 1024 * 1024)
NT = (((1,), (1,)), ((), ()))


def partner(value, axis, apart):
    return lax.ppermute(value, axis, [(i, i ^ 1 << apart) for i in range(lax.axis_size(axis))])


def lanes(index, size):
    return pl.ds(pl.multiple_of(index * size, size), size)


def for_slots(bounds, tables, product, store):
    def batch(width, start):
        def body(step, carry):
            first = start + step * width
            entries = [tuple(table[first + k] for table in tables) for k in range(width)]
            values = [product(*entry) for entry in entries]
            for entry, value in zip(entries, values):
                store(*entry, value)
            return carry

        return body

    first, last = bounds
    groups = (last - first) // GROUP
    middle = first + groups * GROUP
    lax.fori_loop(0, groups, batch(GROUP, first), 0)
    lax.fori_loop(0, (last - middle) // TAIL, batch(TAIL, middle), 0)


def fetch(source_ref, weight_ref, sem):
    slots = source_ref.shape[0]
    share = slots // PARTS
    copies = [
        pltpu.make_async_copy(
            source_ref.at[pl.ds(k * share, share)], weight_ref.at[pl.ds(k * share, share)], sem.at[k]
        )
        for k in range(PARTS)
    ]
    for copy in copies:
        copy.start()
    weight_ref[slots] = jnp.zeros(weight_ref.shape[1:], weight_ref.dtype)
    return copies


def pack_kernel(sends_ref, table_ref, *piece_refs):
    size = piece_refs[0].shape[2]
    for level, piece_ref in enumerate(piece_refs):
        for j in range(piece_ref.shape[0]):
            piece_ref[j] = table_ref[:, lanes(sends_ref[level, j], size)]


def gather_own_kernel(
    own_blocks, rows_ref, cols_ref, count_ref, source_ref, table_ref,
    total_ref, slot_list, row_list, col_list, bound_ref, weight_ref, sem,
):
    copies = fetch(source_ref, weight_ref, sem)
    slots, size, _ = source_ref.shape
    share = slots // PARTS
    count = count_ref[0]
    total_ref[...] = jnp.zeros_like(total_ref)

    def place(slot, state):
        own_at, border_at = state
        col = cols_ref[slot]
        own = col < own_blocks
        at = jnp.where(own, own_at, border_at)
        slot_list[at] = slot
        row_list[at] = rows_ref[slot]
        col_list[at] = jnp.where(own, col, col - own_blocks)
        return jnp.where(own, own_at + 1, own_at), jnp.where(own, border_at, border_at + 1)

    def pad(at):
        for k in range(TAIL - 1):
            slot_list[at + k] = slots
            row_list[at + k] = 0
            col_list[at + k] = 0
        return (at + TAIL - 1) // TAIL * TAIL

    state = (jnp.int32(0), jnp.int32(slots + PARTS * TAIL))
    bound_ref[0, 0], bound_ref[1, 0] = state
    for k in range(PARTS):
        state = lax.fori_loop(
            jnp.minimum(k * share, count), jnp.minimum((k + 1) * share, count), place, state
        )
        state = pad(state[0]), pad(state[1])
        bound_ref[0, k + 1], bound_ref[1, k + 1] = state

    def product(slot, row, col):
        block = table_ref[:, lanes(col, size)]
        return lax.dot_general(block, weight_ref[slot], NT, preferred_element_type=jnp.float32)

    def store(slot, row, col, value):
        total_ref[:, lanes(row, size)] += value

    for k, copy in enumerate(copies):
        copy.wait()
        for_slots((bound_ref[0, k], bound_ref[0, k + 1]), (slot_list, row_list, col_list), product, store)


def gather_border_kernel(
    slot_list, row_list, col_list, bound_ref, source_ref, total_ref, inverse_ref, *rest
):
    *piece_refs, out_ref, weight_ref, border_ref, sum_ref, sem = rest
    copies = fetch(source_ref, weight_ref, sem)
    size = source_ref.shape[1]
    border_size = piece_refs[0].shape[0]
    for level, piece_ref in enumerate(piece_refs):
        border_ref[level * border_size : (level + 1) * border_size] = piece_ref[...]
    sum_ref[...] = total_ref[...]

    def product(slot, row, col):
        return lax.dot_general(
            border_ref[col], weight_ref[slot], NT, preferred_element_type=jnp.float32
        )

    def store(slot, row, col, value):
        sum_ref[:, lanes(row, size)] += value

    for k, copy in enumerate(copies):
        copy.wait()
        for_slots((bound_ref[1, k], bound_ref[1, k + 1]), (slot_list, row_list, col_list), product, store)
    out_ref[...] = (sum_ref[...] * inverse_ref[...]).astype(jnp.bfloat16)


def middle_kernel(
    levels, chunk, own_ref, cross_ref, agg_ref, self_ref, neigh_ref, slab_ref, cot_ref, inverse_ref,
    mixed_ref, direct_ref, scaled_ref, sums_ref,
    all_agg, all_grad, whole_ref, slabs, back_ref, partial_ref, arrived_ref,
    gather_send, gather_recv, slab_send, slab_recv, sum_send, sum_recv,
):
    width, nodes = agg_ref.shape
    steps = nodes // chunk
    me, node = lax.axis_index("feat"), lax.axis_index("nodes")
    near = me + 1 - 2 * (me % 2)
    cross = (me + 2) % 4
    far = 3 - me
    mates = [node + (1 << level) * (1 - 2 * ((node // (1 << level)) % 2)) for level in range(levels)]

    def rows(owner):
        return pl.ds(pl.multiple_of(owner * width, width), width)

    def moved(table, phase, kind, owner, step, target):
        view = table.at[rows(owner), lanes(step, chunk)]
        return pltpu.make_async_remote_copy(
            src_ref=view,
            dst_ref=view,
            send_sem=gather_send.at[phase, kind, step],
            recv_sem=gather_recv.at[phase, kind, step],
            device_id={"feat": target},
            device_id_type=pl.DeviceIdType.MESH,
        )

    def slab(kind, target):
        return pltpu.make_async_remote_copy(
            src_ref=slab_ref.at[target],
            dst_ref=slabs.at[me],
            send_sem=slab_send.at[kind],
            recv_sem=slab_recv.at[kind],
            device_id={"feat": target},
            device_id_type=pl.DeviceIdType.MESH,
        )

    def summed(level):
        return pltpu.make_async_remote_copy(
            src_ref=partial_ref.at[level],
            dst_ref=arrived_ref.at[level],
            send_sem=sum_send.at[level],
            recv_sem=sum_recv.at[level],
            device_id={"nodes": mates[level]},
            device_id_type=pl.DeviceIdType.MESH,
        )

    def share(table, phase, step):
        moved(table, phase, 0, me, step, cross).start()
        moved(table, phase, 1, me, step, near).start()

    def forward(table, phase, step):
        moved(table, phase, 0, cross, step, cross).wait_recv()
        moved(table, phase, 2, cross, step, near).start()

    def complete(table, phase, step):
        moved(table, phase, 1, near, step, near).wait_recv()
        moved(table, phase, 2, far, step, near).wait_recv()

    barrier = pltpu.get_barrier_semaphore()
    for target in (near, cross, far):
        pl.semaphore_signal(
            barrier, inc=1, device_id={"feat": target}, device_id_type=pl.DeviceIdType.MESH
        )
    for mate in mates:
        pl.semaphore_signal(
            barrier, inc=1, device_id={"nodes": mate}, device_id_type=pl.DeviceIdType.MESH
        )
    all_agg[rows(me), :] = agg_ref[...]
    whole_ref[rows(me), :] = own_ref[...]
    whole_ref[rows(cross), :] = cross_ref[...]
    slabs[me] = slab_ref[me]
    partial_ref[0] = jnp.zeros(partial_ref.shape[1:], jnp.float32)
    pl.semaphore_wait(barrier, 3 + levels)

    def share_agg(step, carry):
        share(all_agg, 0, step)
        moved(whole_ref, 2, 1, me, step, near).start()
        moved(whole_ref, 2, 2, cross, step, near).start()
        return carry

    lax.fori_loop(0, steps, share_agg, 0)
    for kind, target in enumerate((near, cross, far)):
        slab(kind, target).start()

    def dense(step):
        complete(whole_ref, 2, step)
        complete(all_agg, 0, step)
        part = lanes(step, chunk)
        whole, agg = whole_ref[:, part], all_agg[:, part]
        values = jnp.dot(self_ref[...], whole, preferred_element_type=jnp.float32) + jnp.dot(
            neigh_ref[...], agg, preferred_element_type=jnp.float32
        )
        square = values * values
        tanh_inner = jnp.tanh(gelu_scale * (values + gelu_cubic * square * values))
        half = 0.5 * (1.0 + tanh_inner)
        mixed_ref[:, part] = (values * half).astype(jnp.bfloat16)
        slope = half + 0.5 * values * (1.0 - tanh_inner * tanh_inner) * gelu_scale * (
            1.0 + 3.0 * gelu_cubic * square
        )
        grad = (cot_ref[:, part].astype(jnp.float32) * slope).astype(jnp.bfloat16)
        all_grad[rows(me), part] = grad
        share(all_grad, 1, step)
        partial_ref[0, 0] += lax.dot_general(grad, whole, NT, preferred_element_type=jnp.float32)
        partial_ref[0, 1] += lax.dot_general(grad, agg, NT, preferred_element_type=jnp.float32)

    def dense_step(step, carry):
        forward(all_agg, 0, step + 1)
        dense(step)
        return carry

    forward(all_agg, 0, 0)
    lax.fori_loop(0, steps - 1, dense_step, 0)
    dense(steps - 1)

    for kind, target in enumerate((near, cross, far)):
        slab(kind, target).wait_recv()
    back_ref[...] = slabs[...].reshape(back_ref.shape[1], back_ref.shape[0]).T

    def project(step):
        complete(all_grad, 1, step)
        part = lanes(step, chunk)
        both = jnp.dot(back_ref[...], all_grad[:, part], preferred_element_type=jnp.float32)
        direct_ref[:, part] = both[:width]
        scaled_ref[:, part] = (both[width:] * inverse_ref[:, part]).astype(jnp.bfloat16)

    def project_step(step, carry):
        forward(all_grad, 1, step + 1)
        project(step)
        return carry

    forward(all_grad, 1, 0)
    for level in range(levels):
        summed(level).start()
        lax.fori_loop(
            level * (steps - 1) // levels, (level + 1) * (steps - 1) // levels, project_step, 0
        )
        summed(level).wait_recv()
        partial_ref[level + 1] = partial_ref[level] + arrived_ref[level]
    sums_ref[...] = partial_ref[levels]
    project(steps - 1)

    def finish(step, carry):
        for phase, table in enumerate((all_agg, all_grad)):
            moved(table, phase, 0, me, step, cross).wait_send()
            moved(table, phase, 1, me, step, near).wait_send()
            moved(table, phase, 2, cross, step, near).wait_send()
        moved(whole_ref, 2, 1, me, step, near).wait_send()
        moved(whole_ref, 2, 2, cross, step, near).wait_send()
        return carry

    lax.fori_loop(0, steps, finish, 0)
    for kind, target in enumerate((near, cross, far)):
        slab(kind, target).wait_send()
    for level in range(levels):
        summed(level).wait_send()


def spread_border_kernel(slot_list, row_list, col_list, bound_ref, source_ref, scaled_ref, *rest):
    *piece_refs, weight_ref, border_ref, sem = rest
    copies = fetch(source_ref, weight_ref, sem)
    size = source_ref.shape[1]
    border_ref[...] = jnp.zeros_like(border_ref)

    def product(slot, row, col):
        block = scaled_ref[:, lanes(row, size)]
        return jnp.dot(block, weight_ref[slot], preferred_element_type=jnp.float32)

    def store(slot, row, col, value):
        border_ref[col] += value

    for k, copy in enumerate(copies):
        copy.wait()
        for_slots((bound_ref[1, k], bound_ref[1, k + 1]), (slot_list, row_list, col_list), product, store)
    border_size = piece_refs[0].shape[0]
    for level, piece_ref in enumerate(piece_refs):
        piece_ref[...] = border_ref[level * border_size : (level + 1) * border_size].astype(jnp.bfloat16)


def spread_own_kernel(
    slot_list, row_list, col_list, bound_ref, source_ref, scaled_ref, direct_ref, total_ref, weight_ref, sem
):
    copies = fetch(source_ref, weight_ref, sem)
    size = source_ref.shape[1]
    total_ref[...] = direct_ref[...]

    def product(slot, row, col):
        block = scaled_ref[:, lanes(row, size)]
        return jnp.dot(block, weight_ref[slot], preferred_element_type=jnp.float32)

    def store(slot, row, col, value):
        total_ref[:, lanes(col, size)] += value

    for k, copy in enumerate(copies):
        copy.wait()
        for_slots((bound_ref[0, k], bound_ref[0, k + 1]), (slot_list, row_list, col_list), product, store)


def collect_kernel(sends_ref, total_ref, *rest):
    piece_refs, out_ref, sum_ref = rest[:-2], rest[-2], rest[-1]
    size = piece_refs[0].shape[2]
    sum_ref[...] = total_ref[...]
    for level, piece_ref in enumerate(piece_refs):
        for j in range(piece_ref.shape[0]):
            sum_ref[:, lanes(sends_ref[level, j], size)] += piece_ref[j].astype(jnp.float32)
    out_ref[...] = sum_ref[...].astype(jnp.bfloat16)


def local(
    features,
    degrees,
    edge_weights,
    block_rows,
    block_cols,
    block_counts,
    send_lists,
    w_self,
    w_neigh,
    cotangent,
):
    row_count, width = features.shape
    slot_count, size, _ = edge_weights.shape
    own_blocks = row_count // size
    border_size = send_lists.shape[2]
    levels = send_lists.shape[1]
    hidden = w_self.shape[0]
    shape = jax.ShapeDtypeStruct
    bf16, f32, i32 = jnp.bfloat16, jnp.float32, jnp.int32
    piece = shape((border_size, width, size), bf16)
    inverse = (1.0 / degrees.astype(f32))[None, :]
    own = features.T
    cross = partner(own, "feat", 1)
    groups = hidden // width
    slab = jnp.concatenate(
        [w.T.reshape(width, groups, width).transpose(1, 0, 2) for w in (w_self, w_neigh)], axis=2
    )
    sends = send_lists[0]

    pieces = pl.pallas_call(
        pack_kernel,
        out_shape=[piece] * levels,
        in_specs=[SMEM, VMEM],
        out_specs=[VMEM] * levels,
        compiler_params=PARAMS,
        name="pack",
    )(sends, own)
    arrived = [partner(value, "nodes", level) for level, value in enumerate(pieces)]
    listed = shape((2 * (slot_count + PARTS * TAIL),), i32)
    weight = pltpu.VMEM((slot_count + 1, size, size), bf16)
    sem = pltpu.SemaphoreType.DMA((PARTS,))
    total, *tables = pl.pallas_call(
        functools.partial(gather_own_kernel, own_blocks),
        out_shape=[shape((width, row_count), f32), listed, listed, listed, shape((2, PARTS + 1), i32)],
        in_specs=[SMEM] * 3 + [ANY, VMEM],
        out_specs=[VMEM] + [SMEM] * 4,
        scratch_shapes=[weight, sem],
        compiler_params=PARAMS,
        cost_estimate=pl.CostEstimate(flops=4 * 10**9, bytes_accessed=12 * 10**6, transcendentals=0),
        name="gather_own",
    )(block_rows, block_cols, block_counts, edge_weights, own)
    aggregated = pl.pallas_call(
        gather_border_kernel,
        out_shape=shape((width, row_count), bf16),
        in_specs=[SMEM] * 4 + [ANY] + [VMEM] * (2 + levels),
        out_specs=VMEM,
        scratch_shapes=[
            weight,
            pltpu.VMEM((levels * border_size, width, size), bf16),
            pltpu.VMEM((width, row_count), f32),
            sem,
        ],
        compiler_params=PARAMS,
        name="gather_border",
    )(*tables, edge_weights, total, inverse, *arrived)

    chunk = 8 * size
    steps = row_count // chunk
    dma = pltpu.SemaphoreType.DMA
    mixed, direct, scaled, sums = pl.pallas_call(
        functools.partial(middle_kernel, levels, chunk),
        out_shape=[
            shape((width, row_count), bf16),
            shape((width, row_count), f32),
            shape((width, row_count), bf16),
            shape((2, width, hidden), f32),
        ],
        in_specs=[VMEM] * 8,
        out_specs=[VMEM] * 4,
        scratch_shapes=[
            pltpu.VMEM((hidden, row_count), bf16),
            pltpu.VMEM((hidden, row_count), bf16),
            pltpu.VMEM((hidden, row_count), bf16),
            pltpu.VMEM((groups, width, 2 * width), bf16),
            pltpu.VMEM((2 * width, hidden), bf16),
            pltpu.VMEM((levels + 1, 2, width, hidden), f32),
            pltpu.VMEM((levels, 2, width, hidden), f32),
            dma((3, 3, steps)),
            dma((3, 3, steps)),
            dma((3,)),
            dma((3,)),
            dma((levels,)),
            dma((levels,)),
        ],
        compiler_params=pltpu.CompilerParams(
            vmem_limit_bytes=56 * 1024 * 1024, collective_id=0, has_side_effects=True
        ),
        name="middle",
    )(own, cross, aggregated, w_self.T, w_neigh.T, slab, cotangent.T, inverse)
    grad_self, grad_neigh = sums[0], sums[1]

    pieces = pl.pallas_call(
        spread_border_kernel,
        out_shape=[piece] * levels,
        in_specs=[SMEM] * 4 + [ANY, VMEM],
        out_specs=[VMEM] * levels,
        scratch_shapes=[weight, pltpu.VMEM((levels * border_size, width, size), f32), sem],
        compiler_params=PARAMS,
        name="spread_border",
    )(*tables, edge_weights, scaled)
    returned = [partner(value, "nodes", level) for level, value in enumerate(pieces)]
    total = pl.pallas_call(
        spread_own_kernel,
        out_shape=shape((width, row_count), f32),
        in_specs=[SMEM] * 4 + [ANY] + [VMEM] * 2,
        out_specs=VMEM,
        scratch_shapes=[weight, sem],
        compiler_params=PARAMS,
        cost_estimate=pl.CostEstimate(flops=4 * 10**9, bytes_accessed=12 * 10**6, transcendentals=0),
        name="spread_own",
    )(*tables, edge_weights, scaled, direct)
    grad_features = pl.pallas_call(
        collect_kernel,
        out_shape=shape((width, row_count), bf16),
        in_specs=[SMEM] + [VMEM] * (1 + levels),
        out_specs=VMEM,
        scratch_shapes=[pltpu.VMEM((width, row_count), f32)],
        compiler_params=PARAMS,
        name="collect",
    )(sends, total, *returned)
    return (mixed.T, grad_features.T, grad_self.T, grad_neigh.T)


def solution(mesh):
    in_specs = (
        P("nodes", "feat"),
        P("nodes"),
        P("nodes", None, None),
        P("nodes"),
        P("nodes"),
        P("nodes"),
        P("nodes", None, None),
        P(None, "feat"),
        P(None, "feat"),
        P("nodes", "feat"),
    )
    out_specs = (P("nodes", "feat"), P("nodes", "feat"), P(None, "feat"), P(None, "feat"))
    return jax.shard_map(local, mesh=mesh, in_specs=in_specs, out_specs=out_specs, check_vma=False)
```

```python
import functools

import jax
import jax.numpy as jnp
from jax import lax
from jax.experimental import pallas as pl
from jax.experimental.pallas import tpu as pltpu
from jax.sharding import PartitionSpec as P

gelu_scale = 0.7978845608028654
gelu_cubic = 0.044715
GROUP = 16
TAIL = 4
PARTS = 4
SMEM = pl.BlockSpec(memory_space=pltpu.SMEM)
VMEM = pl.BlockSpec(memory_space=pltpu.VMEM)
ANY = pl.BlockSpec(memory_space=pl.ANY)
PARAMS = pltpu.CompilerParams(vmem_limit_bytes=24 * 1024 * 1024)
NT = (((1,), (1,)), ((), ()))


def partner(value, axis, apart):
    return lax.ppermute(value, axis, [(i, i ^ 1 << apart) for i in range(lax.axis_size(axis))])


def lanes(index, size):
    return pl.ds(pl.multiple_of(index * size, size), size)


def for_slots(bounds, tables, product, store):
    def batch(width, start):
        def body(step, carry):
            first = start + step * width
            entries = [tuple(table[first + k] for table in tables) for k in range(width)]
            values = [product(*entry) for entry in entries]
            for entry, value in zip(entries, values):
                store(*entry, value)
            return carry

        return body

    first, last = bounds
    groups = (last - first) // GROUP
    middle = first + groups * GROUP
    lax.fori_loop(0, groups, batch(GROUP, first), 0)
    lax.fori_loop(0, (last - middle) // TAIL, batch(TAIL, middle), 0)


def fetch(source_ref, weight_ref, sem):
    slots = source_ref.shape[0]
    share = slots // PARTS
    copies = [
        pltpu.make_async_copy(
            source_ref.at[pl.ds(k * share, share)], weight_ref.at[pl.ds(k * share, share)], sem.at[k]
        )
        for k in range(PARTS)
    ]
    for copy in copies:
        copy.start()
    weight_ref[slots] = jnp.zeros(weight_ref.shape[1:], weight_ref.dtype)
    return copies


def load_pieces(total_ref, sum_ref, piece_refs, border_ref, sem):
    border_size = piece_refs[0].shape[0]
    loads = [pltpu.make_async_copy(total_ref, sum_ref, sem.at[len(piece_refs)])]
    for level, piece_ref in enumerate(piece_refs):
        part = border_ref.at[pl.ds(level * border_size, border_size)]
        loads.append(pltpu.make_async_copy(piece_ref, part, sem.at[level]))
    for load in loads:
        load.start()
    return loads


def pack_kernel(sends_ref, table_ref, *piece_refs):
    size = piece_refs[0].shape[2]
    for level, piece_ref in enumerate(piece_refs):
        for j in range(piece_ref.shape[0]):
            piece_ref[j] = table_ref[:, lanes(sends_ref[level, 0, j], size)]


def gather_own_kernel(
    own_blocks, rows_ref, cols_ref, count_ref, source_ref, table_ref,
    total_ref, slot_list, row_list, col_list, bound_ref, weight_ref, sem,
):
    copies = fetch(source_ref, weight_ref, sem)
    slots, size, _ = source_ref.shape
    share = slots // PARTS
    count = count_ref[0]
    total_ref[...] = jnp.zeros_like(total_ref)

    def place(slot, state):
        own_at, border_at = state
        col = cols_ref[slot]
        own = col < own_blocks
        at = jnp.where(own, own_at, border_at)
        slot_list[at] = slot
        row_list[at] = rows_ref[slot]
        col_list[at] = jnp.where(own, col, col - own_blocks)
        return jnp.where(own, own_at + 1, own_at), jnp.where(own, border_at, border_at + 1)

    def pad(at):
        for k in range(TAIL - 1):
            slot_list[at + k] = slots
            row_list[at + k] = 0
            col_list[at + k] = 0
        return (at + TAIL - 1) // TAIL * TAIL

    state = (jnp.int32(0), jnp.int32(slots + PARTS * TAIL))
    bound_ref[0, 0], bound_ref[1, 0] = state
    for k in range(PARTS):
        state = lax.fori_loop(
            jnp.minimum(k * share, count), jnp.minimum((k + 1) * share, count), place, state
        )
        state = pad(state[0]), pad(state[1])
        bound_ref[0, k + 1], bound_ref[1, k + 1] = state

    def product(slot, row, col):
        block = table_ref[:, lanes(col, size)]
        return lax.dot_general(block, weight_ref[slot], NT, preferred_element_type=jnp.float32)

    def store(slot, row, col, value):
        total_ref[:, lanes(row, size)] += value

    for k, copy in enumerate(copies):
        copy.wait()
        for_slots((bound_ref[0, k], bound_ref[0, k + 1]), (slot_list, row_list, col_list), product, store)


def gather_border_kernel(
    slot_list, row_list, col_list, bound_ref, source_ref, total_ref, degree_ref, *rest
):
    *piece_refs, out_ref, weight_ref, border_ref, sum_ref, sem, load_sem = rest
    loads = load_pieces(total_ref, sum_ref, piece_refs, border_ref, load_sem)
    copies = fetch(source_ref, weight_ref, sem)
    size = source_ref.shape[1]
    for load in loads:
        load.wait()

    def product(slot, row, col):
        return lax.dot_general(
            border_ref[col], weight_ref[slot], NT, preferred_element_type=jnp.float32
        )

    def store(slot, row, col, value):
        sum_ref[:, lanes(row, size)] += value

    for k, copy in enumerate(copies):
        copy.wait()
        for_slots((bound_ref[1, k], bound_ref[1, k + 1]), (slot_list, row_list, col_list), product, store)
    inverse = 1.0 / degree_ref[...].astype(jnp.float32)
    out_ref[...] = (sum_ref[...] * inverse).astype(jnp.bfloat16)


def middle_kernel(
    levels, chunk, own_ref, cross_ref, agg_ref, self_ref, neigh_ref, cot_source, degree_ref,
    mixed_ref, direct_ref, scaled_ref, sums_ref,
    all_agg, all_grad, whole_ref, cot_ref, slab_ref, slabs, back_ref, partial_ref, arrived_ref,
    gather_send, gather_recv, load_sem, slab_send, slab_recv, sum_send, sum_recv,
):
    width, nodes = agg_ref.shape
    steps = nodes // chunk
    me, node = lax.axis_index("feat"), lax.axis_index("nodes")
    near = me + 1 - 2 * (me % 2)
    cross = (me + 2) % 4
    far = 3 - me
    mates = [node + (1 << level) * (1 - 2 * ((node // (1 << level)) % 2)) for level in range(levels)]

    def rows(owner):
        return pl.ds(pl.multiple_of(owner * width, width), width)

    def moved(table, phase, kind, owner, step, target):
        view = table.at[rows(owner), lanes(step, chunk)]
        return pltpu.make_async_remote_copy(
            src_ref=view,
            dst_ref=view,
            send_sem=gather_send.at[phase, kind, step],
            recv_sem=gather_recv.at[phase, kind, step],
            device_id={"feat": target},
            device_id_type=pl.DeviceIdType.MESH,
        )

    def slab(kind, target):
        return pltpu.make_async_remote_copy(
            src_ref=slab_ref.at[target],
            dst_ref=slabs.at[me],
            send_sem=slab_send.at[kind],
            recv_sem=slab_recv.at[kind],
            device_id={"feat": target},
            device_id_type=pl.DeviceIdType.MESH,
        )

    def summed(level):
        return pltpu.make_async_remote_copy(
            src_ref=partial_ref.at[level],
            dst_ref=arrived_ref.at[level],
            send_sem=sum_send.at[level],
            recv_sem=sum_recv.at[level],
            device_id={"nodes": mates[level]},
            device_id_type=pl.DeviceIdType.MESH,
        )

    def share(table, phase, step):
        moved(table, phase, 0, me, step, cross).start()
        moved(table, phase, 1, me, step, near).start()

    def forward(table, phase, step):
        moved(table, phase, 0, cross, step, cross).wait_recv()
        moved(table, phase, 2, cross, step, near).start()

    def complete(table, phase, step):
        moved(table, phase, 1, near, step, near).wait_recv()
        moved(table, phase, 2, far, step, near).wait_recv()

    loads = [
        pltpu.make_async_copy(source, target, load_sem.at[k])
        for k, (source, target) in enumerate(
            (
                (own_ref, whole_ref.at[rows(me), :]),
                (cross_ref, whole_ref.at[rows(cross), :]),
                (cot_source, cot_ref),
            )
        )
    ]
    for load in loads:
        load.start()
    barrier = pltpu.get_barrier_semaphore()
    for target in (near, cross, far):
        pl.semaphore_signal(
            barrier, inc=1, device_id={"feat": target}, device_id_type=pl.DeviceIdType.MESH
        )
    for mate in mates:
        pl.semaphore_signal(
            barrier, inc=1, device_id={"nodes": mate}, device_id_type=pl.DeviceIdType.MESH
        )
    all_agg[rows(me), :] = agg_ref[...]
    for group in range(slab_ref.shape[0]):
        part = slice(group * width, (group + 1) * width)
        slab_ref[group, :, :width] = self_ref[:, part]
        slab_ref[group, :, width:] = neigh_ref[:, part]
    slabs[me] = slab_ref[me]
    partial_ref[0] = jnp.zeros(partial_ref.shape[1:], jnp.float32)
    pl.semaphore_wait(barrier, 3 + levels)

    def share_agg(step, carry):
        share(all_agg, 0, step)
        return carry

    def share_rows(step, carry):
        moved(whole_ref, 2, 1, me, step, near).start()
        moved(whole_ref, 2, 2, cross, step, near).start()
        return carry

    lax.fori_loop(0, steps, share_agg, 0)
    for load in loads:
        load.wait()
    lax.fori_loop(0, steps, share_rows, 0)
    for kind, target in enumerate((near, cross, far)):
        slab(kind, target).start()

    def dense(step):
        complete(whole_ref, 2, step)
        complete(all_agg, 0, step)
        part = lanes(step, chunk)
        whole, agg = whole_ref[:, part], all_agg[:, part]
        values = jnp.dot(self_ref[...], whole, preferred_element_type=jnp.float32) + jnp.dot(
            neigh_ref[...], agg, preferred_element_type=jnp.float32
        )
        square = values * values
        tanh_inner = jnp.tanh(gelu_scale * (values + gelu_cubic * square * values))
        half = 0.5 * (1.0 + tanh_inner)
        mixed_ref[:, part] = (values * half).astype(jnp.bfloat16)
        slope = half + 0.5 * values * (1.0 - tanh_inner * tanh_inner) * gelu_scale * (
            1.0 + 3.0 * gelu_cubic * square
        )
        grad = (cot_ref[:, part].astype(jnp.float32) * slope).astype(jnp.bfloat16)
        all_grad[rows(me), part] = grad
        share(all_grad, 1, step)
        partial_ref[0, 0] += lax.dot_general(grad, whole, NT, preferred_element_type=jnp.float32)
        partial_ref[0, 1] += lax.dot_general(grad, agg, NT, preferred_element_type=jnp.float32)

    def dense_step(step, carry):
        forward(all_agg, 0, step + 1)
        dense(step)
        return carry

    forward(all_agg, 0, 0)
    lax.fori_loop(0, steps - 1, dense_step, 0)
    dense(steps - 1)

    for kind, target in enumerate((near, cross, far)):
        slab(kind, target).wait_recv()
    back_ref[...] = slabs[...].reshape(back_ref.shape[1], back_ref.shape[0]).T

    def project(step):
        complete(all_grad, 1, step)
        part = lanes(step, chunk)
        both = jnp.dot(back_ref[...], all_grad[:, part], preferred_element_type=jnp.float32)
        direct_ref[:, part] = both[:width]
        inverse = 1.0 / degree_ref[:, part].astype(jnp.float32)
        scaled_ref[:, part] = (both[width:] * inverse).astype(jnp.bfloat16)

    def project_step(step, carry):
        forward(all_grad, 1, step + 1)
        project(step)
        return carry

    forward(all_grad, 1, 0)
    for level in range(levels):
        summed(level).start()
        lax.fori_loop(
            level * (steps - 1) // levels, (level + 1) * (steps - 1) // levels, project_step, 0
        )
        summed(level).wait_recv()
        partial_ref[level + 1] = partial_ref[level] + arrived_ref[level]
    sums_ref[...] = partial_ref[levels]
    project(steps - 1)

    def finish(step, carry):
        for phase, table in enumerate((all_agg, all_grad)):
            moved(table, phase, 0, me, step, cross).wait_send()
            moved(table, phase, 1, me, step, near).wait_send()
            moved(table, phase, 2, cross, step, near).wait_send()
        moved(whole_ref, 2, 1, me, step, near).wait_send()
        moved(whole_ref, 2, 2, cross, step, near).wait_send()
        return carry

    lax.fori_loop(0, steps, finish, 0)
    for kind, target in enumerate((near, cross, far)):
        slab(kind, target).wait_send()
    for level in range(levels):
        summed(level).wait_send()


def spread_border_kernel(slot_list, row_list, col_list, bound_ref, source_ref, scaled_ref, *rest):
    *piece_refs, weight_ref, border_ref, sem = rest
    copies = fetch(source_ref, weight_ref, sem)
    size = source_ref.shape[1]
    border_ref[...] = jnp.zeros_like(border_ref)

    def product(slot, row, col):
        block = scaled_ref[:, lanes(row, size)]
        return jnp.dot(block, weight_ref[slot], preferred_element_type=jnp.float32)

    def store(slot, row, col, value):
        border_ref[col] += value

    for k, copy in enumerate(copies):
        copy.wait()
        for_slots((bound_ref[1, k], bound_ref[1, k + 1]), (slot_list, row_list, col_list), product, store)
    border_size = piece_refs[0].shape[0]
    for level, piece_ref in enumerate(piece_refs):
        piece_ref[...] = border_ref[level * border_size : (level + 1) * border_size].astype(jnp.bfloat16)


def spread_own_kernel(
    slot_list, row_list, col_list, bound_ref, source_ref, scaled_ref, direct_ref, total_ref, weight_ref, sem, load_sem
):
    load = pltpu.make_async_copy(direct_ref, total_ref, load_sem.at[0])
    load.start()
    copies = fetch(source_ref, weight_ref, sem)
    size = source_ref.shape[1]
    load.wait()

    def product(slot, row, col):
        block = scaled_ref[:, lanes(row, size)]
        return jnp.dot(block, weight_ref[slot], preferred_element_type=jnp.float32)

    def store(slot, row, col, value):
        total_ref[:, lanes(col, size)] += value

    for k, copy in enumerate(copies):
        copy.wait()
        for_slots((bound_ref[0, k], bound_ref[0, k + 1]), (slot_list, row_list, col_list), product, store)


def collect_kernel(sends_ref, total_ref, *rest):
    *piece_refs, out_ref, sum_ref, border_ref, load_sem = rest
    border_size, _, size = piece_refs[0].shape
    for load in load_pieces(total_ref, sum_ref, piece_refs, border_ref, load_sem):
        load.wait()
    for level in range(len(piece_refs)):
        for j in range(border_size):
            block = border_ref[level * border_size + j].astype(jnp.float32)
            sum_ref[:, lanes(sends_ref[level, 0, j], size)] += block
    out_ref[...] = sum_ref[...].astype(jnp.bfloat16)


def local(
    features,
    degrees,
    edge_weights,
    block_rows,
    block_cols,
    block_counts,
    send_lists,
    w_self,
    w_neigh,
    cotangent,
):
    row_count, width = features.shape
    slot_count, size, _ = edge_weights.shape
    own_blocks = row_count // size
    border_size = send_lists.shape[2]
    levels = send_lists.shape[1]
    hidden = w_self.shape[0]
    shape = jax.ShapeDtypeStruct
    bf16, f32, i32 = jnp.bfloat16, jnp.float32, jnp.int32
    piece = shape((border_size, width, size), bf16)
    degree = degrees[None, :]
    own = features.T
    cross = partner(own, "feat", 1)
    groups = hidden // width
    sends = send_lists.transpose(1, 0, 2)

    pieces = pl.pallas_call(
        pack_kernel,
        out_shape=[piece] * levels,
        in_specs=[SMEM, VMEM],
        out_specs=[VMEM] * levels,
        compiler_params=PARAMS,
        name="pack",
    )(sends, own)
    arrived = [partner(pieces[level], "nodes", level) for level in reversed(range(levels))][::-1]
    listed = shape((2 * (slot_count + PARTS * TAIL),), i32)
    weight = pltpu.VMEM((slot_count + 1, size, size), bf16)
    sem = pltpu.SemaphoreType.DMA((PARTS,))
    load_sem = pltpu.SemaphoreType.DMA((levels + 1,))
    total, *tables = pl.pallas_call(
        functools.partial(gather_own_kernel, own_blocks),
        out_shape=[shape((width, row_count), f32), listed, listed, listed, shape((2, PARTS + 1), i32)],
        in_specs=[SMEM] * 3 + [ANY, VMEM],
        out_specs=[VMEM] + [SMEM] * 4,
        scratch_shapes=[weight, sem],
        compiler_params=PARAMS,
        cost_estimate=pl.CostEstimate(flops=4 * 10**9, bytes_accessed=12 * 10**6, transcendentals=0),
        name="gather_own",
    )(block_rows, block_cols, block_counts, edge_weights, own)
    aggregated = pl.pallas_call(
        gather_border_kernel,
        out_shape=shape((width, row_count), bf16),
        in_specs=[SMEM] * 4 + [ANY, ANY, VMEM] + [ANY] * levels,
        out_specs=VMEM,
        scratch_shapes=[
            weight,
            pltpu.VMEM((levels * border_size, width, size), bf16),
            pltpu.VMEM((width, row_count), f32),
            sem,
            load_sem,
        ],
        compiler_params=PARAMS,
        name="gather_border",
    )(*tables, edge_weights, total, degree, *arrived)

    chunk = 4 * size
    steps = row_count // chunk
    dma = pltpu.SemaphoreType.DMA
    mixed, direct, scaled, sums = pl.pallas_call(
        functools.partial(middle_kernel, levels, chunk),
        out_shape=[
            shape((width, row_count), bf16),
            shape((width, row_count), f32),
            shape((width, row_count), bf16),
            shape((2, width, hidden), f32),
        ],
        in_specs=[ANY, ANY, VMEM, VMEM, VMEM, ANY, VMEM],
        out_specs=[VMEM] * 4,
        scratch_shapes=[
            pltpu.VMEM((hidden, row_count), bf16),
            pltpu.VMEM((hidden, row_count), bf16),
            pltpu.VMEM((hidden, row_count), bf16),
            pltpu.VMEM((width, row_count), bf16),
            pltpu.VMEM((groups, width, 2 * width), bf16),
            pltpu.VMEM((groups, width, 2 * width), bf16),
            pltpu.VMEM((2 * width, hidden), bf16),
            pltpu.VMEM((levels + 1, 2, width, hidden), f32),
            pltpu.VMEM((levels, 2, width, hidden), f32),
            dma((3, 3, steps)),
            dma((3, 3, steps)),
            dma((3,)),
            dma((3,)),
            dma((3,)),
            dma((levels,)),
            dma((levels,)),
        ],
        compiler_params=pltpu.CompilerParams(
            vmem_limit_bytes=40 * 1024 * 1024, collective_id=0, has_side_effects=True
        ),
        name="middle",
    )(own, cross, aggregated, w_self.T, w_neigh.T, cotangent.T, degree)
    grad_self, grad_neigh = sums[0], sums[1]

    pieces = pl.pallas_call(
        spread_border_kernel,
        out_shape=[piece] * levels,
        in_specs=[SMEM] * 4 + [ANY, VMEM],
        out_specs=[VMEM] * levels,
        scratch_shapes=[weight, pltpu.VMEM((levels * border_size, width, size), f32), sem],
        compiler_params=PARAMS,
        name="spread_border",
    )(*tables, edge_weights, scaled)
    returned = [partner(pieces[level], "nodes", level) for level in reversed(range(levels))][::-1]
    total = pl.pallas_call(
        spread_own_kernel,
        out_shape=shape((width, row_count), f32),
        in_specs=[SMEM] * 4 + [ANY, VMEM, ANY],
        out_specs=VMEM,
        scratch_shapes=[weight, sem, load_sem],
        compiler_params=PARAMS,
        cost_estimate=pl.CostEstimate(flops=4 * 10**9, bytes_accessed=12 * 10**6, transcendentals=0),
        name="spread_own",
    )(*tables, edge_weights, scaled, direct)
    grad_features = pl.pallas_call(
        collect_kernel,
        out_shape=shape((width, row_count), bf16),
        in_specs=[SMEM] + [ANY] * (1 + levels),
        out_specs=VMEM,
        scratch_shapes=[
            pltpu.VMEM((width, row_count), f32),
            pltpu.VMEM((levels * border_size, width, size), bf16),
            load_sem,
        ],
        compiler_params=PARAMS,
        name="collect",
    )(sends, total, *returned)
    return (mixed.T, grad_features.T, grad_self.T, grad_neigh.T)


def solution(mesh):
    in_specs = (
        P("nodes", "feat"),
        P("nodes"),
        P("nodes", None, None),
        P("nodes"),
        P("nodes"),
        P("nodes"),
        P("nodes", None, None),
        P(None, "feat"),
        P(None, "feat"),
        P("nodes", "feat"),
    )
    out_specs = (P("nodes", "feat"), P("nodes", "feat"), P(None, "feat"), P(None, "feat"))
    return jax.shard_map(local, mesh=mesh, in_specs=in_specs, out_specs=out_specs, check_vma=False)
```

```python
import functools

import jax
import jax.numpy as jnp
from jax import lax
from jax.experimental import pallas as pl
from jax.experimental.pallas import tpu as pltpu
from jax.sharding import PartitionSpec as P

gelu_scale = 0.7978845608028654
gelu_cubic = 0.044715
GROUP = 16
TAIL = 4
PARTS = 4
SMEM = pl.BlockSpec(memory_space=pltpu.SMEM)
VMEM = pl.BlockSpec(memory_space=pltpu.VMEM)
ANY = pl.BlockSpec(memory_space=pl.ANY)
PARAMS = pltpu.CompilerParams(vmem_limit_bytes=24 * 1024 * 1024)
NT = (((1,), (1,)), ((), ()))


def partner(value, axis, apart):
    return lax.ppermute(value, axis, [(i, i ^ 1 << apart) for i in range(lax.axis_size(axis))])


def lanes(index, size):
    return pl.ds(pl.multiple_of(index * size, size), size)


def for_slots(bounds, tables, product, store):
    def batch(width, start):
        def body(step, carry):
            first = start + step * width
            entries = [tuple(table[first + k] for table in tables) for k in range(width)]
            values = [product(*entry) for entry in entries]
            for entry, value in zip(entries, values):
                store(*entry, value)
            return carry

        return body

    first, last = bounds
    groups = (last - first) // GROUP
    middle = first + groups * GROUP
    lax.fori_loop(0, groups, batch(GROUP, first), 0)
    lax.fori_loop(0, (last - middle) // TAIL, batch(TAIL, middle), 0)


def fetch(source_ref, weight_ref, sem):
    slots = source_ref.shape[0]
    share = slots // PARTS
    copies = [
        pltpu.make_async_copy(
            source_ref.at[pl.ds(k * share, share)], weight_ref.at[pl.ds(k * share, share)], sem.at[k]
        )
        for k in range(PARTS)
    ]
    for copy in copies:
        copy.start()
    weight_ref[slots] = jnp.zeros(weight_ref.shape[1:], weight_ref.dtype)
    return copies


def load_pieces(total_ref, sum_ref, piece_refs, border_ref, sem):
    border_size = piece_refs[0].shape[0]
    loads = [pltpu.make_async_copy(total_ref, sum_ref, sem.at[len(piece_refs)])]
    for level, piece_ref in enumerate(piece_refs):
        part = border_ref.at[pl.ds(level * border_size, border_size)]
        loads.append(pltpu.make_async_copy(piece_ref, part, sem.at[level]))
    for load in loads:
        load.start()
    return loads


def pack_kernel(sends_ref, source_ref, *rest):
    *piece_refs, table_ref, sem = rest
    load = pltpu.make_async_copy(source_ref, table_ref, sem)
    load.start()
    load.wait()
    size = piece_refs[0].shape[2]
    for level, piece_ref in enumerate(piece_refs):
        for j in range(piece_ref.shape[0]):
            piece_ref[j] = table_ref[:, lanes(sends_ref[level, 0, j], size)]


def gather_own_kernel(
    own_blocks, rows_ref, cols_ref, count_ref, source_ref, table_source,
    total_ref, slot_list, row_list, col_list, bound_ref, weight_ref, table_ref, sem, load_sem,
):
    load = pltpu.make_async_copy(table_source, table_ref, load_sem.at[0])
    load.start()
    copies = fetch(source_ref, weight_ref, sem)
    slots, size, _ = source_ref.shape
    share = slots // PARTS
    count = count_ref[0]
    total_ref[...] = jnp.zeros_like(total_ref)

    def place(slot, state):
        own_at, border_at = state
        col = cols_ref[slot]
        own = col < own_blocks
        at = jnp.where(own, own_at, border_at)
        slot_list[at] = slot
        row_list[at] = rows_ref[slot]
        col_list[at] = jnp.where(own, col, col - own_blocks)
        return jnp.where(own, own_at + 1, own_at), jnp.where(own, border_at, border_at + 1)

    def pad(at):
        for k in range(TAIL - 1):
            slot_list[at + k] = slots
            row_list[at + k] = 0
            col_list[at + k] = 0
        return (at + TAIL - 1) // TAIL * TAIL

    state = (jnp.int32(0), jnp.int32(slots + PARTS * TAIL))
    bound_ref[0, 0], bound_ref[1, 0] = state
    for k in range(PARTS):
        state = lax.fori_loop(
            jnp.minimum(k * share, count), jnp.minimum((k + 1) * share, count), place, state
        )
        state = pad(state[0]), pad(state[1])
        bound_ref[0, k + 1], bound_ref[1, k + 1] = state

    def product(slot, row, col):
        block = table_ref[:, lanes(col, size)]
        return lax.dot_general(block, weight_ref[slot], NT, preferred_element_type=jnp.float32)

    def store(slot, row, col, value):
        total_ref[:, lanes(row, size)] += value

    load.wait()
    for k, copy in enumerate(copies):
        copy.wait()
        for_slots((bound_ref[0, k], bound_ref[0, k + 1]), (slot_list, row_list, col_list), product, store)


def gather_border_kernel(
    slot_list, row_list, col_list, bound_ref, source_ref, total_ref, degree_ref, *rest
):
    *piece_refs, out_ref, weight_ref, border_ref, sum_ref, sem, load_sem = rest
    loads = load_pieces(total_ref, sum_ref, piece_refs, border_ref, load_sem)
    copies = fetch(source_ref, weight_ref, sem)
    size = source_ref.shape[1]
    for load in loads:
        load.wait()

    def product(slot, row, col):
        return lax.dot_general(
            border_ref[col], weight_ref[slot], NT, preferred_element_type=jnp.float32
        )

    def store(slot, row, col, value):
        sum_ref[:, lanes(row, size)] += value

    for k, copy in enumerate(copies):
        copy.wait()
        for_slots((bound_ref[1, k], bound_ref[1, k + 1]), (slot_list, row_list, col_list), product, store)
    inverse = 1.0 / degree_ref[...].astype(jnp.float32)
    out_ref[...] = (sum_ref[...] * inverse).astype(jnp.bfloat16)


def middle_kernel(
    levels, chunk, own_ref, cross_ref, agg_ref, self_ref, neigh_ref, cot_source, degree_ref,
    mixed_ref, direct_ref, scaled_ref, sums_ref,
    all_agg, all_grad, whole_ref, cot_ref, slab_ref, slabs, back_ref, partial_ref, arrived_ref,
    gather_send, gather_recv, load_sem, slab_send, slab_recv, sum_send, sum_recv,
):
    width, nodes = agg_ref.shape
    steps = nodes // chunk
    me, node = lax.axis_index("feat"), lax.axis_index("nodes")
    near = me + 1 - 2 * (me % 2)
    cross = (me + 2) % 4
    far = 3 - me
    mates = [node + (1 << level) * (1 - 2 * ((node // (1 << level)) % 2)) for level in range(levels)]

    def rows(owner):
        return pl.ds(pl.multiple_of(owner * width, width), width)

    def moved(table, phase, kind, owner, step, target):
        view = table.at[rows(owner), lanes(step, chunk)]
        return pltpu.make_async_remote_copy(
            src_ref=view,
            dst_ref=view,
            send_sem=gather_send.at[phase, kind, step],
            recv_sem=gather_recv.at[phase, kind, step],
            device_id={"feat": target},
            device_id_type=pl.DeviceIdType.MESH,
        )

    def slab(kind, target):
        return pltpu.make_async_remote_copy(
            src_ref=slab_ref.at[target],
            dst_ref=slabs.at[me],
            send_sem=slab_send.at[kind],
            recv_sem=slab_recv.at[kind],
            device_id={"feat": target},
            device_id_type=pl.DeviceIdType.MESH,
        )

    def summed(level):
        return pltpu.make_async_remote_copy(
            src_ref=partial_ref.at[level],
            dst_ref=arrived_ref.at[level],
            send_sem=sum_send.at[level],
            recv_sem=sum_recv.at[level],
            device_id={"nodes": mates[level]},
            device_id_type=pl.DeviceIdType.MESH,
        )

    def share(table, phase, step):
        moved(table, phase, 0, me, step, cross).start()
        moved(table, phase, 1, me, step, near).start()

    def forward(table, phase, step):
        moved(table, phase, 0, cross, step, cross).wait_recv()
        moved(table, phase, 2, cross, step, near).start()

    def complete(table, phase, step):
        moved(table, phase, 1, near, step, near).wait_recv()
        moved(table, phase, 2, far, step, near).wait_recv()

    loads = [
        pltpu.make_async_copy(source, target, load_sem.at[k])
        for k, (source, target) in enumerate(
            (
                (own_ref, whole_ref.at[rows(me), :]),
                (cross_ref, whole_ref.at[rows(cross), :]),
                (cot_source, cot_ref),
            )
        )
    ]
    for load in loads:
        load.start()
    barrier = pltpu.get_barrier_semaphore()
    for target in (near, cross, far):
        pl.semaphore_signal(
            barrier, inc=1, device_id={"feat": target}, device_id_type=pl.DeviceIdType.MESH
        )
    for mate in mates:
        pl.semaphore_signal(
            barrier, inc=1, device_id={"nodes": mate}, device_id_type=pl.DeviceIdType.MESH
        )
    all_agg[rows(me), :] = agg_ref[...]
    for group in range(slab_ref.shape[0]):
        part = slice(group * width, (group + 1) * width)
        slab_ref[group, :, :width] = self_ref[:, part]
        slab_ref[group, :, width:] = neigh_ref[:, part]
    slabs[me] = slab_ref[me]
    partial_ref[0] = jnp.zeros(partial_ref.shape[1:], jnp.float32)
    pl.semaphore_wait(barrier, 3 + levels)

    def share_agg(step, carry):
        share(all_agg, 0, step)
        return carry

    def share_rows(step, carry):
        moved(whole_ref, 2, 1, me, step, near).start()
        moved(whole_ref, 2, 2, cross, step, near).start()
        return carry

    lax.fori_loop(0, steps, share_agg, 0)
    for load in loads:
        load.wait()
    lax.fori_loop(0, steps, share_rows, 0)
    for kind, target in enumerate((near, cross, far)):
        slab(kind, target).start()

    def dense(step):
        complete(whole_ref, 2, step)
        complete(all_agg, 0, step)
        part = lanes(step, chunk)
        whole, agg = whole_ref[:, part], all_agg[:, part]
        values = jnp.dot(self_ref[...], whole, preferred_element_type=jnp.float32) + jnp.dot(
            neigh_ref[...], agg, preferred_element_type=jnp.float32
        )
        square = values * values
        tanh_inner = jnp.tanh(gelu_scale * (values + gelu_cubic * square * values))
        half = 0.5 * (1.0 + tanh_inner)
        mixed_ref[:, part] = (values * half).astype(jnp.bfloat16)
        slope = half + 0.5 * values * (1.0 - tanh_inner * tanh_inner) * gelu_scale * (
            1.0 + 3.0 * gelu_cubic * square
        )
        grad = (cot_ref[:, part].astype(jnp.float32) * slope).astype(jnp.bfloat16)
        all_grad[rows(me), part] = grad
        share(all_grad, 1, step)
        partial_ref[0, 0] += lax.dot_general(grad, whole, NT, preferred_element_type=jnp.float32)
        partial_ref[0, 1] += lax.dot_general(grad, agg, NT, preferred_element_type=jnp.float32)

    def dense_step(step, carry):
        forward(all_agg, 0, step + 1)
        dense(step)
        return carry

    forward(all_agg, 0, 0)
    lax.fori_loop(0, steps - 1, dense_step, 0)
    dense(steps - 1)

    for kind, target in enumerate((near, cross, far)):
        slab(kind, target).wait_recv()
    back_ref[...] = slabs[...].reshape(back_ref.shape[1], back_ref.shape[0]).T

    def project(step):
        complete(all_grad, 1, step)
        part = lanes(step, chunk)
        both = jnp.dot(back_ref[...], all_grad[:, part], preferred_element_type=jnp.float32)
        direct_ref[:, part] = both[:width]
        inverse = 1.0 / degree_ref[:, part].astype(jnp.float32)
        scaled_ref[:, part] = (both[width:] * inverse).astype(jnp.bfloat16)

    def project_step(step, carry):
        forward(all_grad, 1, step + 1)
        project(step)
        return carry

    forward(all_grad, 1, 0)
    for level in range(levels):
        summed(level).start()
        lax.fori_loop(
            level * (steps - 1) // levels, (level + 1) * (steps - 1) // levels, project_step, 0
        )
        summed(level).wait_recv()
        partial_ref[level + 1] = partial_ref[level] + arrived_ref[level]
    sums_ref[...] = partial_ref[levels]
    project(steps - 1)

    def finish(step, carry):
        for phase, table in enumerate((all_agg, all_grad)):
            moved(table, phase, 0, me, step, cross).wait_send()
            moved(table, phase, 1, me, step, near).wait_send()
            moved(table, phase, 2, cross, step, near).wait_send()
        moved(whole_ref, 2, 1, me, step, near).wait_send()
        moved(whole_ref, 2, 2, cross, step, near).wait_send()
        return carry

    lax.fori_loop(0, steps, finish, 0)
    for kind, target in enumerate((near, cross, far)):
        slab(kind, target).wait_send()
    for level in range(levels):
        summed(level).wait_send()


def spread_border_kernel(slot_list, row_list, col_list, bound_ref, source_ref, scaled_ref, *rest):
    *piece_refs, weight_ref, border_ref, sem = rest
    copies = fetch(source_ref, weight_ref, sem)
    size = source_ref.shape[1]
    border_ref[...] = jnp.zeros_like(border_ref)

    def product(slot, row, col):
        block = scaled_ref[:, lanes(row, size)]
        return jnp.dot(block, weight_ref[slot], preferred_element_type=jnp.float32)

    def store(slot, row, col, value):
        border_ref[col] += value

    for k, copy in enumerate(copies):
        copy.wait()
        for_slots((bound_ref[1, k], bound_ref[1, k + 1]), (slot_list, row_list, col_list), product, store)
    border_size = piece_refs[0].shape[0]
    for level, piece_ref in enumerate(piece_refs):
        piece_ref[...] = border_ref[level * border_size : (level + 1) * border_size].astype(jnp.bfloat16)


def spread_own_kernel(
    slot_list, row_list, col_list, bound_ref, source_ref, scaled_ref, direct_ref, mixed_ref,
    total_ref, copied_ref, weight_ref, sem, load_sem,
):
    copy_mixed = pltpu.make_async_copy(mixed_ref, copied_ref, load_sem.at[1])
    copy_mixed.start()
    load = pltpu.make_async_copy(direct_ref, total_ref, load_sem.at[0])
    load.start()
    copies = fetch(source_ref, weight_ref, sem)
    size = source_ref.shape[1]
    load.wait()

    def product(slot, row, col):
        block = scaled_ref[:, lanes(row, size)]
        return jnp.dot(block, weight_ref[slot], preferred_element_type=jnp.float32)

    def store(slot, row, col, value):
        total_ref[:, lanes(col, size)] += value

    for k, copy in enumerate(copies):
        copy.wait()
        for_slots((bound_ref[0, k], bound_ref[0, k + 1]), (slot_list, row_list, col_list), product, store)
    copy_mixed.wait()


def collect_kernel(sends_ref, total_ref, *rest):
    *piece_refs, out_ref, sum_ref, border_ref, load_sem = rest
    border_size, _, size = piece_refs[0].shape
    for load in load_pieces(total_ref, sum_ref, piece_refs, border_ref, load_sem):
        load.wait()
    for level in range(len(piece_refs)):
        for j in range(border_size):
            block = border_ref[level * border_size + j].astype(jnp.float32)
            sum_ref[:, lanes(sends_ref[level, 0, j], size)] += block
    out_ref[...] = sum_ref[...].astype(jnp.bfloat16)


def local(
    features,
    degrees,
    edge_weights,
    block_rows,
    block_cols,
    block_counts,
    send_lists,
    w_self,
    w_neigh,
    cotangent,
):
    row_count, width = features.shape
    slot_count, size, _ = edge_weights.shape
    own_blocks = row_count // size
    border_size = send_lists.shape[2]
    levels = send_lists.shape[1]
    hidden = w_self.shape[0]
    shape = jax.ShapeDtypeStruct
    bf16, f32, i32 = jnp.bfloat16, jnp.float32, jnp.int32
    piece = shape((border_size, width, size), bf16)
    degree = degrees[None, :]
    own = features.T
    cross = partner(own, "feat", 1)
    groups = hidden // width
    sends = send_lists.transpose(1, 0, 2)

    pieces = pl.pallas_call(
        pack_kernel,
        out_shape=[piece] * levels,
        in_specs=[SMEM, ANY],
        out_specs=[VMEM] * levels,
        scratch_shapes=[pltpu.VMEM((width, row_count), bf16), pltpu.SemaphoreType.DMA],
        compiler_params=pltpu.CompilerParams(vmem_limit_bytes=60 * 1024 * 1024),
        name="pack",
    )(sends, own)
    arrived = [partner(pieces[level], "nodes", level) for level in reversed(range(levels))][::-1]
    listed = shape((2 * (slot_count + PARTS * TAIL),), i32)
    weight = pltpu.VMEM((slot_count + 1, size, size), bf16)
    sem = pltpu.SemaphoreType.DMA((PARTS,))
    load_sem = pltpu.SemaphoreType.DMA((levels + 1,))
    total, *tables = pl.pallas_call(
        functools.partial(gather_own_kernel, own_blocks),
        out_shape=[shape((width, row_count), f32), listed, listed, listed, shape((2, PARTS + 1), i32)],
        in_specs=[SMEM] * 3 + [ANY, ANY],
        out_specs=[VMEM] + [SMEM] * 4,
        scratch_shapes=[weight, pltpu.VMEM((width, row_count), bf16), sem, load_sem],
        compiler_params=pltpu.CompilerParams(vmem_limit_bytes=46 * 1024 * 1024),
        cost_estimate=pl.CostEstimate(flops=4 * 10**9, bytes_accessed=12 * 10**6, transcendentals=0),
        name="gather_own",
    )(block_rows, block_cols, block_counts, edge_weights, own)
    aggregated = pl.pallas_call(
        gather_border_kernel,
        out_shape=shape((width, row_count), bf16),
        in_specs=[SMEM] * 4 + [ANY, ANY, VMEM] + [ANY] * levels,
        out_specs=VMEM,
        scratch_shapes=[
            weight,
            pltpu.VMEM((levels * border_size, width, size), bf16),
            pltpu.VMEM((width, row_count), f32),
            sem,
            load_sem,
        ],
        compiler_params=PARAMS,
        name="gather_border",
    )(*tables, edge_weights, total, degree, *arrived)

    chunk = 4 * size
    steps = row_count // chunk
    dma = pltpu.SemaphoreType.DMA
    mixed, direct, scaled, sums = pl.pallas_call(
        functools.partial(middle_kernel, levels, chunk),
        out_shape=[
            shape((width, row_count), bf16),
            shape((width, row_count), f32),
            shape((width, row_count), bf16),
            shape((2, width, hidden), f32),
        ],
        in_specs=[ANY, ANY, VMEM, VMEM, VMEM, ANY, VMEM],
        out_specs=[VMEM] * 4,
        scratch_shapes=[
            pltpu.VMEM((hidden, row_count), bf16),
            pltpu.VMEM((hidden, row_count), bf16),
            pltpu.VMEM((hidden, row_count), bf16),
            pltpu.VMEM((width, row_count), bf16),
            pltpu.VMEM((groups, width, 2 * width), bf16),
            pltpu.VMEM((groups, width, 2 * width), bf16),
            pltpu.VMEM((2 * width, hidden), bf16),
            pltpu.VMEM((levels + 1, 2, width, hidden), f32),
            pltpu.VMEM((levels, 2, width, hidden), f32),
            dma((3, 3, steps)),
            dma((3, 3, steps)),
            dma((3,)),
            dma((3,)),
            dma((3,)),
            dma((levels,)),
            dma((levels,)),
        ],
        compiler_params=pltpu.CompilerParams(
            vmem_limit_bytes=40 * 1024 * 1024, collective_id=0, has_side_effects=True
        ),
        name="middle",
    )(own, cross, aggregated, w_self.T, w_neigh.T, cotangent.T, degree)
    grad_self, grad_neigh = sums[0], sums[1]

    pieces = pl.pallas_call(
        spread_border_kernel,
        out_shape=[piece] * levels,
        in_specs=[SMEM] * 4 + [ANY, VMEM],
        out_specs=[VMEM] * levels,
        scratch_shapes=[weight, pltpu.VMEM((levels * border_size, width, size), f32), sem],
        compiler_params=PARAMS,
        name="spread_border",
    )(*tables, edge_weights, scaled)
    returned = [partner(pieces[level], "nodes", level) for level in reversed(range(levels))][::-1]
    total, mixed = pl.pallas_call(
        spread_own_kernel,
        out_shape=[shape((width, row_count), f32), shape((width, row_count), bf16)],
        in_specs=[SMEM] * 4 + [ANY, VMEM, ANY, ANY],
        out_specs=[VMEM, ANY],
        scratch_shapes=[weight, sem, load_sem],
        compiler_params=PARAMS,
        cost_estimate=pl.CostEstimate(flops=4 * 10**9, bytes_accessed=12 * 10**6, transcendentals=0),
        name="spread_own",
    )(*tables, edge_weights, scaled, direct, mixed)
    grad_features = pl.pallas_call(
        collect_kernel,
        out_shape=shape((width, row_count), bf16),
        in_specs=[SMEM] + [ANY] * (1 + levels),
        out_specs=VMEM,
        scratch_shapes=[
            pltpu.VMEM((width, row_count), f32),
            pltpu.VMEM((levels * border_size, width, size), bf16),
            load_sem,
        ],
        compiler_params=PARAMS,
        name="collect",
    )(sends, total, *returned)
    return (mixed.T, grad_features.T, grad_self.T, grad_neigh.T)


def solution(mesh):
    in_specs = (
        P("nodes", "feat"),
        P("nodes"),
        P("nodes", None, None),
        P("nodes"),
        P("nodes"),
        P("nodes"),
        P("nodes", None, None),
        P(None, "feat"),
        P(None, "feat"),
        P("nodes", "feat"),
    )
    out_specs = (P("nodes", "feat"), P("nodes", "feat"), P(None, "feat"), P(None, "feat"))
    return jax.shard_map(local, mesh=mesh, in_specs=in_specs, out_specs=out_specs, check_vma=False)
```

```python
import functools

import jax
import jax.numpy as jnp
from jax import lax
from jax.experimental import pallas as pl
from jax.experimental.pallas import tpu as pltpu
from jax.sharding import PartitionSpec as P

gelu_scale = 0.7978845608028654
gelu_cubic = 0.044715
GROUP = 16
TAIL = 4
PARTS = 4
SMEM = pl.BlockSpec(memory_space=pltpu.SMEM)
VMEM = pl.BlockSpec(memory_space=pltpu.VMEM)
ANY = pl.BlockSpec(memory_space=pl.ANY)
PARAMS = pltpu.CompilerParams(vmem_limit_bytes=24 * 1024 * 1024)
NT = (((1,), (1,)), ((), ()))


def partner(value, axis, apart):
    return lax.ppermute(value, axis, [(i, i ^ 1 << apart) for i in range(lax.axis_size(axis))])


def lanes(index, size):
    return pl.ds(pl.multiple_of(index * size, size), size)


def for_slots(bounds, tables, product, store):
    def batch(width, start):
        def body(step, carry):
            first = start + step * width
            entries = [tuple(table[first + k] for table in tables) for k in range(width)]
            values = [product(*entry) for entry in entries]
            for entry, value in zip(entries, values):
                store(*entry, value)
            return carry

        return body

    first, last = bounds
    groups = (last - first) // GROUP
    middle = first + groups * GROUP
    lax.fori_loop(0, groups, batch(GROUP, first), 0)
    lax.fori_loop(0, (last - middle) // TAIL, batch(TAIL, middle), 0)


def fetch(source_ref, weight_ref, sem):
    slots = source_ref.shape[0]
    share = slots // PARTS
    copies = [
        pltpu.make_async_copy(
            source_ref.at[pl.ds(k * share, share)], weight_ref.at[pl.ds(k * share, share)], sem.at[k]
        )
        for k in range(PARTS)
    ]
    for copy in copies:
        copy.start()
    weight_ref[slots] = jnp.zeros(weight_ref.shape[1:], weight_ref.dtype)
    return copies


def load_pieces(total_ref, sum_ref, piece_refs, border_ref, sem):
    border_size = piece_refs[0].shape[0]
    loads = [pltpu.make_async_copy(total_ref, sum_ref, sem.at[len(piece_refs)])]
    for level, piece_ref in enumerate(piece_refs):
        part = border_ref.at[pl.ds(level * border_size, border_size)]
        loads.append(pltpu.make_async_copy(piece_ref, part, sem.at[level]))
    for load in loads:
        load.start()
    return loads


def pack_kernel(sends_ref, source_ref, *rest):
    *piece_refs, table_ref, sem = rest
    load = pltpu.make_async_copy(source_ref, table_ref, sem)
    load.start()
    load.wait()
    size = piece_refs[0].shape[2]
    for level, piece_ref in enumerate(piece_refs):
        for j in range(piece_ref.shape[0]):
            piece_ref[j] = table_ref[:, lanes(sends_ref[level, 0, j], size)]


def gather_own_kernel(
    own_blocks, rows_ref, cols_ref, count_ref, source_ref, table_source,
    total_ref, slot_list, row_list, col_list, bound_ref, weight_ref, table_ref, sem, load_sem,
):
    load = pltpu.make_async_copy(table_source, table_ref, load_sem.at[0])
    load.start()
    copies = fetch(source_ref, weight_ref, sem)
    slots, size, _ = source_ref.shape
    share = slots // PARTS
    count = count_ref[0]
    total_ref[...] = jnp.zeros_like(total_ref)

    def place(slot, state):
        own_at, border_at = state
        col = cols_ref[slot]
        own = col < own_blocks
        at = jnp.where(own, own_at, border_at)
        slot_list[at] = slot
        row_list[at] = rows_ref[slot]
        col_list[at] = jnp.where(own, col, col - own_blocks)
        return jnp.where(own, own_at + 1, own_at), jnp.where(own, border_at, border_at + 1)

    def pad(at):
        for k in range(TAIL - 1):
            slot_list[at + k] = slots
            row_list[at + k] = 0
            col_list[at + k] = 0
        return (at + TAIL - 1) // TAIL * TAIL

    state = (jnp.int32(0), jnp.int32(slots + PARTS * TAIL))
    bound_ref[0, 0], bound_ref[1, 0] = state
    for k in range(PARTS):
        state = lax.fori_loop(
            jnp.minimum(k * share, count), jnp.minimum((k + 1) * share, count), place, state
        )
        state = pad(state[0]), pad(state[1])
        bound_ref[0, k + 1], bound_ref[1, k + 1] = state

    def product(slot, row, col):
        block = table_ref[:, lanes(col, size)]
        return lax.dot_general(block, weight_ref[slot], NT, preferred_element_type=jnp.float32)

    def store(slot, row, col, value):
        total_ref[:, lanes(row, size)] += value

    load.wait()
    for k, copy in enumerate(copies):
        copy.wait()
        for_slots((bound_ref[0, k], bound_ref[0, k + 1]), (slot_list, row_list, col_list), product, store)


def gather_border_kernel(
    slot_list, row_list, col_list, bound_ref, source_ref, total_ref, degree_ref, *rest
):
    *piece_refs, out_ref, weight_ref, border_ref, sum_ref, sem, load_sem = rest
    loads = load_pieces(total_ref, sum_ref, piece_refs, border_ref, load_sem)
    copies = fetch(source_ref, weight_ref, sem)
    size = source_ref.shape[1]
    for load in loads:
        load.wait()

    def product(slot, row, col):
        return lax.dot_general(
            border_ref[col], weight_ref[slot], NT, preferred_element_type=jnp.float32
        )

    def store(slot, row, col, value):
        sum_ref[:, lanes(row, size)] += value

    for k, copy in enumerate(copies):
        copy.wait()
        for_slots((bound_ref[1, k], bound_ref[1, k + 1]), (slot_list, row_list, col_list), product, store)
    inverse = 1.0 / degree_ref[...].astype(jnp.float32)
    out_ref[...] = (sum_ref[...] * inverse).astype(jnp.bfloat16)


def middle_kernel(
    levels, chunk, own_ref, cross_ref, agg_ref, self_ref, neigh_ref, cot_source, degree_ref,
    mixed_ref, direct_ref, scaled_ref, sums_ref,
    all_agg, all_grad, whole_ref, cot_ref, slab_ref, slabs, back_ref, partial_ref, arrived_ref,
    gather_send, gather_recv, load_sem, slab_send, slab_recv, sum_send, sum_recv,
):
    width, nodes = agg_ref.shape
    steps = nodes // chunk
    me, node = lax.axis_index("feat"), lax.axis_index("nodes")
    near = me + 1 - 2 * (me % 2)
    cross = (me + 2) % 4
    far = 3 - me
    mates = [node + (1 << level) * (1 - 2 * ((node // (1 << level)) % 2)) for level in range(levels)]

    def rows(owner):
        return pl.ds(pl.multiple_of(owner * width, width), width)

    def moved(table, phase, kind, owner, step, target):
        view = table.at[rows(owner), lanes(step, chunk)]
        return pltpu.make_async_remote_copy(
            src_ref=view,
            dst_ref=view,
            send_sem=gather_send.at[phase, kind, step],
            recv_sem=gather_recv.at[phase, kind, step],
            device_id={"feat": target},
            device_id_type=pl.DeviceIdType.MESH,
        )

    def slab(kind, target):
        return pltpu.make_async_remote_copy(
            src_ref=slab_ref.at[target],
            dst_ref=slabs.at[me],
            send_sem=slab_send.at[kind],
            recv_sem=slab_recv.at[kind],
            device_id={"feat": target},
            device_id_type=pl.DeviceIdType.MESH,
        )

    def summed(level):
        return pltpu.make_async_remote_copy(
            src_ref=partial_ref.at[level],
            dst_ref=arrived_ref.at[level],
            send_sem=sum_send.at[level],
            recv_sem=sum_recv.at[level],
            device_id={"nodes": mates[level]},
            device_id_type=pl.DeviceIdType.MESH,
        )

    def share(table, phase, step):
        moved(table, phase, 0, me, step, cross).start()
        moved(table, phase, 1, me, step, near).start()

    def forward(table, phase, step):
        moved(table, phase, 0, cross, step, cross).wait_recv()
        moved(table, phase, 2, cross, step, near).start()

    def complete(table, phase, step):
        moved(table, phase, 1, near, step, near).wait_recv()
        moved(table, phase, 2, far, step, near).wait_recv()

    loads = [
        pltpu.make_async_copy(source, target, load_sem.at[k])
        for k, (source, target) in enumerate(
            (
                (own_ref, whole_ref.at[rows(me), :]),
                (cross_ref, whole_ref.at[rows(cross), :]),
                (cot_source, cot_ref),
            )
        )
    ]
    for load in loads:
        load.start()
    barrier = pltpu.get_barrier_semaphore()
    for target in (near, cross, far):
        pl.semaphore_signal(
            barrier, inc=1, device_id={"feat": target}, device_id_type=pl.DeviceIdType.MESH
        )
    for mate in mates:
        pl.semaphore_signal(
            barrier, inc=1, device_id={"nodes": mate}, device_id_type=pl.DeviceIdType.MESH
        )
    all_agg[rows(me), :] = agg_ref[...]
    pl.semaphore_wait(barrier, 3 + levels)

    def share_agg(step, carry):
        share(all_agg, 0, step)
        return carry

    def share_rows(step, carry):
        moved(whole_ref, 2, 1, me, step, near).start()
        moved(whole_ref, 2, 2, cross, step, near).start()
        return carry

    lax.fori_loop(0, steps, share_agg, 0)
    for group in range(slab_ref.shape[0]):
        part = slice(group * width, (group + 1) * width)
        slab_ref[group, :, :width] = self_ref[:, part]
        slab_ref[group, :, width:] = neigh_ref[:, part]
    slabs[me] = slab_ref[me]
    partial_ref[0] = jnp.zeros(partial_ref.shape[1:], jnp.float32)
    for load in loads:
        load.wait()
    lax.fori_loop(0, steps, share_rows, 0)
    for kind, target in enumerate((near, cross, far)):
        slab(kind, target).start()

    def dense(step):
        complete(whole_ref, 2, step)
        complete(all_agg, 0, step)
        part = lanes(step, chunk)
        whole, agg = whole_ref[:, part], all_agg[:, part]
        values = jnp.dot(self_ref[...], whole, preferred_element_type=jnp.float32) + jnp.dot(
            neigh_ref[...], agg, preferred_element_type=jnp.float32
        )
        square = values * values
        tanh_inner = jnp.tanh(gelu_scale * (values + gelu_cubic * square * values))
        half = 0.5 * (1.0 + tanh_inner)
        mixed_ref[:, part] = (values * half).astype(jnp.bfloat16)
        slope = half + 0.5 * values * (1.0 - tanh_inner * tanh_inner) * gelu_scale * (
            1.0 + 3.0 * gelu_cubic * square
        )
        grad = (cot_ref[:, part].astype(jnp.float32) * slope).astype(jnp.bfloat16)
        all_grad[rows(me), part] = grad
        share(all_grad, 1, step)
        partial_ref[0, 0] += lax.dot_general(grad, whole, NT, preferred_element_type=jnp.float32)
        partial_ref[0, 1] += lax.dot_general(grad, agg, NT, preferred_element_type=jnp.float32)

    def dense_step(step, carry):
        forward(all_agg, 0, step + 1)
        dense(step)
        return carry

    forward(all_agg, 0, 0)
    lax.fori_loop(0, steps - 1, dense_step, 0)
    dense(steps - 1)

    for kind, target in enumerate((near, cross, far)):
        slab(kind, target).wait_recv()
    back_ref[...] = slabs[...].reshape(back_ref.shape[1], back_ref.shape[0]).T

    def project(step):
        complete(all_grad, 1, step)
        part = lanes(step, chunk)
        both = jnp.dot(back_ref[...], all_grad[:, part], preferred_element_type=jnp.float32)
        direct_ref[:, part] = both[:width]
        inverse = 1.0 / degree_ref[:, part].astype(jnp.float32)
        scaled_ref[:, part] = (both[width:] * inverse).astype(jnp.bfloat16)

    def project_step(step, carry):
        forward(all_grad, 1, step + 1)
        project(step)
        return carry

    forward(all_grad, 1, 0)
    for level in range(levels):
        summed(level).start()
        lax.fori_loop(
            level * (steps - 1) // levels, (level + 1) * (steps - 1) // levels, project_step, 0
        )
        summed(level).wait_recv()
        partial_ref[level + 1] = partial_ref[level] + arrived_ref[level]
    sums_ref[...] = partial_ref[levels]
    project(steps - 1)

    def finish(step, carry):
        for phase, table in enumerate((all_agg, all_grad)):
            moved(table, phase, 0, me, step, cross).wait_send()
            moved(table, phase, 1, me, step, near).wait_send()
            moved(table, phase, 2, cross, step, near).wait_send()
        moved(whole_ref, 2, 1, me, step, near).wait_send()
        moved(whole_ref, 2, 2, cross, step, near).wait_send()
        return carry

    lax.fori_loop(0, steps, finish, 0)
    for kind, target in enumerate((near, cross, far)):
        slab(kind, target).wait_send()
    for level in range(levels):
        summed(level).wait_send()


def spread_border_kernel(slot_list, row_list, col_list, bound_ref, source_ref, scaled_ref, *rest):
    *piece_refs, weight_ref, border_ref, sem = rest
    copies = fetch(source_ref, weight_ref, sem)
    size = source_ref.shape[1]
    border_ref[...] = jnp.zeros_like(border_ref)

    def product(slot, row, col):
        block = scaled_ref[:, lanes(row, size)]
        return jnp.dot(block, weight_ref[slot], preferred_element_type=jnp.float32)

    def store(slot, row, col, value):
        border_ref[col] += value

    for k, copy in enumerate(copies):
        copy.wait()
        for_slots((bound_ref[1, k], bound_ref[1, k + 1]), (slot_list, row_list, col_list), product, store)
    border_size = piece_refs[0].shape[0]
    for level, piece_ref in enumerate(piece_refs):
        piece_ref[...] = border_ref[level * border_size : (level + 1) * border_size].astype(jnp.bfloat16)


def spread_own_kernel(
    slot_list, row_list, col_list, bound_ref, source_ref, scaled_ref, direct_ref, mixed_ref,
    total_ref, copied_ref, weight_ref, sem, load_sem,
):
    copy_mixed = pltpu.make_async_copy(mixed_ref, copied_ref, load_sem.at[1])
    copy_mixed.start()
    load = pltpu.make_async_copy(direct_ref, total_ref, load_sem.at[0])
    load.start()
    copies = fetch(source_ref, weight_ref, sem)
    size = source_ref.shape[1]
    load.wait()

    def product(slot, row, col):
        block = scaled_ref[:, lanes(row, size)]
        return jnp.dot(block, weight_ref[slot], preferred_element_type=jnp.float32)

    def store(slot, row, col, value):
        total_ref[:, lanes(col, size)] += value

    for k, copy in enumerate(copies):
        copy.wait()
        for_slots((bound_ref[0, k], bound_ref[0, k + 1]), (slot_list, row_list, col_list), product, store)
    copy_mixed.wait()


def collect_kernel(sends_ref, total_ref, *rest):
    *piece_refs, out_ref, sum_ref, border_ref, load_sem = rest
    border_size, _, size = piece_refs[0].shape
    for load in load_pieces(total_ref, sum_ref, piece_refs, border_ref, load_sem):
        load.wait()
    for level in range(len(piece_refs)):
        for j in range(border_size):
            block = border_ref[level * border_size + j].astype(jnp.float32)
            sum_ref[:, lanes(sends_ref[level, 0, j], size)] += block
    out_ref[...] = sum_ref[...].astype(jnp.bfloat16)


def local(
    features,
    degrees,
    edge_weights,
    block_rows,
    block_cols,
    block_counts,
    send_lists,
    w_self,
    w_neigh,
    cotangent,
):
    row_count, width = features.shape
    slot_count, size, _ = edge_weights.shape
    own_blocks = row_count // size
    border_size = send_lists.shape[2]
    levels = send_lists.shape[1]
    hidden = w_self.shape[0]
    shape = jax.ShapeDtypeStruct
    bf16, f32, i32 = jnp.bfloat16, jnp.float32, jnp.int32
    piece = shape((border_size, width, size), bf16)
    degree = degrees[None, :]
    own = features.T
    cross = partner(own, "feat", 1)
    groups = hidden // width
    sends = send_lists.transpose(1, 0, 2)

    pieces = pl.pallas_call(
        pack_kernel,
        out_shape=[piece] * levels,
        in_specs=[SMEM, ANY],
        out_specs=[VMEM] * levels,
        scratch_shapes=[pltpu.VMEM((width, row_count), bf16), pltpu.SemaphoreType.DMA],
        compiler_params=pltpu.CompilerParams(vmem_limit_bytes=60 * 1024 * 1024),
        name="pack",
    )(sends, own)
    arrived = [partner(pieces[level], "nodes", level) for level in reversed(range(levels))][::-1]
    listed = shape((2 * (slot_count + PARTS * TAIL),), i32)
    weight = pltpu.VMEM((slot_count + 1, size, size), bf16)
    sem = pltpu.SemaphoreType.DMA((PARTS,))
    load_sem = pltpu.SemaphoreType.DMA((levels + 1,))
    total, *tables = pl.pallas_call(
        functools.partial(gather_own_kernel, own_blocks),
        out_shape=[shape((width, row_count), f32), listed, listed, listed, shape((2, PARTS + 1), i32)],
        in_specs=[SMEM] * 3 + [ANY, ANY],
        out_specs=[VMEM] + [SMEM] * 4,
        scratch_shapes=[weight, pltpu.VMEM((width, row_count), bf16), sem, load_sem],
        compiler_params=pltpu.CompilerParams(vmem_limit_bytes=46 * 1024 * 1024),
        cost_estimate=pl.CostEstimate(flops=4 * 10**9, bytes_accessed=12 * 10**6, transcendentals=0),
        name="gather_own",
    )(block_rows, block_cols, block_counts, edge_weights, own)
    aggregated = pl.pallas_call(
        gather_border_kernel,
        out_shape=shape((width, row_count), bf16),
        in_specs=[SMEM] * 4 + [ANY, ANY, VMEM] + [ANY] * levels,
        out_specs=VMEM,
        scratch_shapes=[
            weight,
            pltpu.VMEM((levels * border_size, width, size), bf16),
            pltpu.VMEM((width, row_count), f32),
            sem,
            load_sem,
        ],
        compiler_params=PARAMS,
        name="gather_border",
    )(*tables, edge_weights, total, degree, *arrived)

    chunk = 4 * size
    steps = row_count // chunk
    dma = pltpu.SemaphoreType.DMA
    mixed, direct, scaled, sums = pl.pallas_call(
        functools.partial(middle_kernel, levels, chunk),
        out_shape=[
            shape((width, row_count), bf16),
            shape((width, row_count), f32),
            shape((width, row_count), bf16),
            shape((2, width, hidden), f32),
        ],
        in_specs=[ANY, ANY, VMEM, VMEM, VMEM, ANY, VMEM],
        out_specs=[VMEM] * 4,
        scratch_shapes=[
            pltpu.VMEM((hidden, row_count), bf16),
            pltpu.VMEM((hidden, row_count), bf16),
            pltpu.VMEM((hidden, row_count), bf16),
            pltpu.VMEM((width, row_count), bf16),
            pltpu.VMEM((groups, width, 2 * width), bf16),
            pltpu.VMEM((groups, width, 2 * width), bf16),
            pltpu.VMEM((2 * width, hidden), bf16),
            pltpu.VMEM((levels + 1, 2, width, hidden), f32),
            pltpu.VMEM((levels, 2, width, hidden), f32),
            dma((3, 3, steps)),
            dma((3, 3, steps)),
            dma((3,)),
            dma((3,)),
            dma((3,)),
            dma((levels,)),
            dma((levels,)),
        ],
        compiler_params=pltpu.CompilerParams(
            vmem_limit_bytes=40 * 1024 * 1024, collective_id=0, has_side_effects=True
        ),
        name="middle",
    )(own, cross, aggregated, w_self.T, w_neigh.T, cotangent.T, degree)
    grad_self, grad_neigh = sums[0], sums[1]

    pieces = pl.pallas_call(
        spread_border_kernel,
        out_shape=[piece] * levels,
        in_specs=[SMEM] * 4 + [ANY, VMEM],
        out_specs=[VMEM] * levels,
        scratch_shapes=[weight, pltpu.VMEM((levels * border_size, width, size), f32), sem],
        compiler_params=PARAMS,
        name="spread_border",
    )(*tables, edge_weights, scaled)
    returned = [partner(pieces[level], "nodes", level) for level in reversed(range(levels))][::-1]
    total, mixed = pl.pallas_call(
        spread_own_kernel,
        out_shape=[shape((width, row_count), f32), shape((width, row_count), bf16)],
        in_specs=[SMEM] * 4 + [ANY, VMEM, ANY, ANY],
        out_specs=[VMEM, ANY],
        scratch_shapes=[weight, sem, load_sem],
        compiler_params=PARAMS,
        cost_estimate=pl.CostEstimate(flops=4 * 10**9, bytes_accessed=12 * 10**6, transcendentals=0),
        name="spread_own",
    )(*tables, edge_weights, scaled, direct, mixed)
    grad_features = pl.pallas_call(
        collect_kernel,
        out_shape=shape((width, row_count), bf16),
        in_specs=[SMEM] + [ANY] * (1 + levels),
        out_specs=VMEM,
        scratch_shapes=[
            pltpu.VMEM((width, row_count), f32),
            pltpu.VMEM((levels * border_size, width, size), bf16),
            load_sem,
        ],
        compiler_params=PARAMS,
        name="collect",
    )(sends, total, *returned)
    return (mixed.T, grad_features.T, grad_self.T, grad_neigh.T)


def solution(mesh):
    in_specs = (
        P("nodes", "feat"),
        P("nodes"),
        P("nodes", None, None),
        P("nodes"),
        P("nodes"),
        P("nodes"),
        P("nodes", None, None),
        P(None, "feat"),
        P(None, "feat"),
        P("nodes", "feat"),
    )
    out_specs = (P("nodes", "feat"), P("nodes", "feat"), P(None, "feat"), P(None, "feat"))
    return jax.shard_map(local, mesh=mesh, in_specs=in_specs, out_specs=out_specs, check_vma=False)
```
